128 devices in a mesh: ctx: 8 (over z, core), img: 16 (over y, x).
Axes of the slice: x: 4, y: 4, z: 4, core: 2. Of those that a mesh axis runs over, the one named last changes fastest.
Arguments:
- queries: bfloat16 [16384, 4096], P(('ctx', 'img')), may hold values from -110 to 110
- tile_ids: int32 [16384, 1], P(('ctx', 'img')), may hold values from 0 to 15; in each aligned block of 128 rows (0 to 127, 128 to 255, ...) at most 9 rows name the same one
- keys: bfloat16 [16, 1664, 512], P('img'), may hold values from -6 to 6
- values: bfloat16 [16, 1664, 512], P('img'), may hold values from -6 to 6
- patch_counts: int32 [16], P('img'), may hold values from 801 to 1601, as said below
- output_gradient: bfloat16 [16384, 4096], P(('ctx', 'img')), may hold values from -6 to 6
Outputs:
- attended: bfloat16 [16384, 4096], P(('ctx', 'img'))
- query_grad: bfloat16 [16384, 4096], P(('ctx', 'img'))
- key_grad: float32 [16, 1664, 512], P('img', 'ctx')
- value_grad: float32 [16, 1664, 512], P('img', 'ctx')
The draws below stay inside these ranges and needn't reach their ends.
Inputs may be any that keep to these rules, and one draw needn't show every extreme that they name: `tile_ids`: each token names one tile; among the 128 tokens of one device no tile is named by more than 9 tokens, a bound that some block reaches. `patch_counts`: some tile has all 1601 patches valid.
All inputs are finite; a program needn't handle non-finite values.
Results may differ from the reference program's by a relative error of at most 0.038.
Values may be sent and summed in bfloat16 or wider, within the bound.
No kernel may reach another device: no remote copies, remote signals or barrier semaphores. Data moves between devices by JAX's collectives and lax.ppermute only.
A program may use at most 128 MiB of HBM per device.

```python
import math
import jax
import jax.numpy as jnp
import numpy as np
from jax import lax

HQ = 32
LOCAL_KV_HEADS = 4
HEAD_WIDTH = 128
PATCH = 1601
LIST = 1
TOK_DEV = 128
TOKENS = 16384
IMAGE_TILES = 16
CAP = 9
TILE_PATCH_ROWS = 1664


def draw_queries(key, part):
    key = jax.random.fold_in(key, 11)
    key_one = jax.random.fold_in(key, 0)
    array_shape = (TOKENS, HQ * HEAD_WIDTH)
    drawn = jax.random.truncated_normal(key_one, -6.0, 6.0, array_shape, jnp.float32)
    return drawn.astype(jnp.bfloat16)


def draw_patch_counts(key, part):
    key = jax.random.fold_in(key, 23)
    key_one, key_two = jax.random.split(key, 2)
    counted = jax.random.randint(key_one, (IMAGE_TILES,), PATCH // 2 + 1, PATCH + 1)
    target = jax.random.randint(key_two, (), 0, IMAGE_TILES)
    return jnp.where(jnp.arange(IMAGE_TILES) == target, PATCH, counted).astype(jnp.int32)


def steps_of(stream_key, shape, cuts, smallest, high):
    def one(axis_at, parts):
        steps = jax.random.uniform(jax.random.fold_in(jax.random.fold_in(stream_key, 6), axis_at), (parts,), jnp.float32, smallest / len(cuts), high / len(cuts))
        return jnp.repeat(jnp.exp(steps), shape[axis_at] // parts).reshape((-1,) + (1,) * (len(shape) - axis_at - 1))

    gain = one(*cuts[0])
    for cut in cuts[1:]:
        gain = gain * one(*cut)
    return gain


def assign_block(stream_key, own, number, rows, amount, top, most, lean):
    order = jax.random.permutation(stream_key, amount)
    crowded, ordinary = portions_of(amount, rows * top, most, lean, True), portions_of(amount, rows * top, most, lean, False)
    places = jnp.arange(amount)

    def named(lengths, turn):
        used = int((lengths > 0).sum())
        fixed = max(1, used // 4)
        moved = fixed + (places - fixed + turn * (used - fixed)) % max(1, amount - fixed)
        return jnp.zeros((amount,), jnp.int32).at[order[jnp.where(places < fixed, places, moved)]].set(jnp.asarray(lengths, jnp.int32))

    lengths = jnp.where(number % 4 == 0, named(crowded, number // 4), named(ordinary, number - number // 4 - 1))
    mixed = jax.random.permutation(jax.random.fold_in(own, 3), amount)
    giver, taker = mixed[0:amount // 2 * 2:2], mixed[1:amount // 2 * 2:2]
    margin = jnp.minimum(lengths[giver] - 1, most - lengths[taker]) // 2
    margin = jnp.where((giver == order[0]) | (taker == order[0]) | (lengths[taker] == 0), 0, jnp.maximum(margin, 0))
    moved = jax.random.randint(jax.random.fold_in(own, 4), (amount // 2,), 0, 1 << 20) % (margin + 1)
    lengths = lengths.at[giver].add(-moved).at[taker].add(moved)
    items = jnp.searchsorted(jnp.cumsum(lengths), jnp.arange(rows * top), side="right").astype(jnp.int32)
    listing = items.reshape(top, rows).T
    listing = listing[jax.random.permutation(jax.random.fold_in(own, 1), rows)]
    turn = jax.random.randint(jax.random.fold_in(own, 2), (rows, 1), 0, top)
    return jnp.take_along_axis(listing, (jnp.arange(top)[None, :] + turn) % top, axis=1)


def portions_of(amount, total, reach, skew, full):
    weights = [(1 << 20) // math.isqrt(grade ** skew) + 1 for grade in range(1, amount + 1)]
    largest = reach if full else min(reach, max(-(-total // amount), total * weights[0] // sum(weights)))
    least = 1 if total - largest >= amount - 1 else 0
    given, surplus = [largest] + [least] * (amount - 1), total - largest - least * (amount - 1)
    while surplus > 0:
        free = [i for i in range(1, amount) if given[i] < largest] or [i for i in range(1, amount) if given[i] < reach]
        whole, budget = sum([weights[i] for i in free]), surplus
        for i in free:
            extra = min(reach - given[i], max(1, budget * weights[i] // whole), surplus)
            given[i] = given[i] + extra
            surplus = surplus - extra
    return np.array(given)


def bell_draw(rng, shape, scale, limit, cuts=(), kind=jnp.bfloat16):
    result = scale * jax.random.normal(rng, shape, jnp.float32)
    if cuts:
        result = result * steps_of(rng, shape, cuts, -0.22, 0.18)
    return jnp.clip(result, -limit, limit).astype(kind)


def setup_inputs(seed: int = 0) -> dict:
    splits = jax.random.split(jax.random.key(seed), 7)
    queries = draw_queries(jax.random.fold_in(splits[6], 71), 0)
    tile_ids_keys = jax.random.split(jax.random.fold_in(splits[1], 1), TOKENS // TOK_DEV)
    tile_ids_turns = jax.random.permutation(jax.random.fold_in(splits[1], 3), TOKENS // TOK_DEV)
    tile_ids = jax.vmap(lambda own, number: assign_block(jax.random.fold_in(splits[1], 2), own, number, TOK_DEV, IMAGE_TILES, LIST, CAP, 2))(tile_ids_keys, tile_ids_turns).reshape((TOKENS, LIST))
    keys = bell_draw(splits[2], (IMAGE_TILES, TILE_PATCH_ROWS, LOCAL_KV_HEADS * HEAD_WIDTH), 1.0, 6.0, ((0, 16),))
    values = bell_draw(splits[3], (IMAGE_TILES, TILE_PATCH_ROWS, LOCAL_KV_HEADS * HEAD_WIDTH), 1.0, 6.0, ((0, 16),))
    patch_counts = draw_patch_counts(jax.random.fold_in(splits[6], 71), 0)
    output_gradient = bell_draw(splits[5], (TOKENS, HQ * HEAD_WIDTH), 1.0, 6.0, ((0, 128),))
    return dict(queries=queries, tile_ids=tile_ids, keys=keys, values=values, patch_counts=patch_counts, output_gradient=output_gradient)


def multiply(pattern, left_operand, right_op):
    left_operand, right_op = lax.optimization_barrier((left_operand, right_op))
    return jnp.einsum(pattern, left_operand.astype(jnp.float32), right_op.astype(jnp.float32))

def route_slots(tile_ids, tile_num, capacity):
    onehot = (tile_ids[:, :, None] == jnp.arange(tile_num, dtype=jnp.int32)[None, None, :]).astype(jnp.int32)
    flagged = lax.optimization_barrier(jnp.sum(onehot, axis=1))
    before = jnp.cumsum(flagged, axis=0) - flagged
    slot_of = lax.optimization_barrier(jnp.sum(onehot * before[:, None, :], axis=2))
    return (tile_ids * capacity + slot_of).astype(jnp.int32)

def dispatch_index(flat_slot, total):
    token_num = flat_slot.shape[0]
    owner_ids = jnp.broadcast_to(jnp.arange(token_num, dtype=jnp.int32)[:, None], flat_slot.shape)
    filled = jnp.full((total,), token_num, jnp.int32)
    return filled.at[flat_slot.reshape(-1)].set(owner_ids.reshape(-1))

def padded_take(source, index_map):
    extended = jnp.concatenate([source, jnp.zeros((1,) + source.shape[1:], source.dtype)], axis=0)
    return extended[index_map]

def tile_forward(query_rows, key_tile, value_tile, counts):
    tile_num, row_num, row_width = query_rows.shape
    key_heads = key_tile.shape[2] // HEAD_WIDTH
    group_size = row_width // HEAD_WIDTH // key_heads
    inv_root = 1.0 / math.sqrt(HEAD_WIDTH)
    live_keys = jnp.arange(key_tile.shape[1], dtype=jnp.int32)[None, :] < counts[:, None]
    out_list, max_list, total_list = ([], [], [])
    for head_group in range(key_heads):
        query_start = head_group * group_size * HEAD_WIDTH
        query_part = query_rows[:, :, query_start:query_start + group_size * HEAD_WIDTH].reshape(tile_num, row_num, group_size, HEAD_WIDTH)
        key_part = key_tile[:, :, head_group * HEAD_WIDTH:(head_group + 1) * HEAD_WIDTH]
        value_part = value_tile[:, :, head_group * HEAD_WIDTH:(head_group + 1) * HEAD_WIDTH]
        scores = multiply('trhd,tkd->trhk', query_part, key_part) * inv_root
        scores = jnp.where(live_keys[:, None, None, :], scores, -jnp.inf)
        part_peak = lax.optimization_barrier(jnp.max(scores, axis=3))
        weights = jnp.exp(scores - part_peak[..., None])
        total_list.append(lax.optimization_barrier(jnp.sum(weights, axis=3)))
        max_list.append(part_peak)
        mixed = multiply('trhk,tkd->trhd', weights.astype(jnp.bfloat16), value_part)
        out_list.append(mixed.reshape(tile_num, row_num, group_size * HEAD_WIDTH))
    return (jnp.concatenate(out_list, axis=2), jnp.concatenate(max_list, axis=2), jnp.concatenate(total_list, axis=2))

def tile_backward(query_rows, grad_rows, total_rows, dot_rows, key_tile, value_tile, counts):
    tile_num, row_num, row_width = query_rows.shape
    key_heads = key_tile.shape[2] // HEAD_WIDTH
    group_size = row_width // HEAD_WIDTH // key_heads
    inv_root = 1.0 / math.sqrt(HEAD_WIDTH)
    live_keys = jnp.arange(key_tile.shape[1], dtype=jnp.int32)[None, :] < counts[:, None]
    query_list, key_list, value_list = ([], [], [])
    for head_group in range(key_heads):
        query_start = head_group * group_size * HEAD_WIDTH
        head_start = head_group * group_size
        query_part = query_rows[:, :, query_start:query_start + group_size * HEAD_WIDTH].reshape(tile_num, row_num, group_size, HEAD_WIDTH)
        grad_part = grad_rows[:, :, query_start:query_start + group_size * HEAD_WIDTH].reshape(tile_num, row_num, group_size, HEAD_WIDTH)
        total_part = total_rows[:, :, head_start:head_start + group_size]
        dot_part = dot_rows[:, :, head_start:head_start + group_size]
        key_part = key_tile[:, :, head_group * HEAD_WIDTH:(head_group + 1) * HEAD_WIDTH]
        value_part = value_tile[:, :, head_group * HEAD_WIDTH:(head_group + 1) * HEAD_WIDTH]
        scores = multiply('trhd,tkd->trhk', query_part, key_part) * inv_root
        scores = jnp.where(live_keys[:, None, None, :], scores, -jnp.inf)
        prob_full = jnp.exp(scores - total_part[..., None])
        value_list.append(multiply('trhk,trhd->tkd', prob_full.astype(jnp.bfloat16), grad_part))
        prob_grad = multiply('trhd,tkd->trhk', grad_part, value_part)
        score_grad = (prob_full * (prob_grad - dot_part[..., None])).astype(jnp.bfloat16)
        query_term = multiply('trhk,tkd->trhd', score_grad, key_part) * inv_root
        query_list.append(query_term.reshape(tile_num, row_num, group_size * HEAD_WIDTH))
        key_list.append(multiply('trhk,trhd->tkd', score_grad, query_part) * inv_root)
    return (jnp.concatenate(query_list, axis=2), jnp.concatenate(key_list, axis=2), jnp.concatenate(value_list, axis=2))

def merge_partials(part_out, part_max, part_total):
    token_num = part_out.shape[0]
    highest = lax.optimization_barrier(jnp.max(part_max, axis=1))
    factor = jnp.exp(part_max - highest[:, None, :])
    denominator = lax.optimization_barrier(jnp.sum(factor * part_total, axis=1))
    heads_out = part_out.reshape(token_num, LIST, HQ, HEAD_WIDTH)
    numerator = lax.optimization_barrier(jnp.sum(factor[..., None] * heads_out, axis=1))
    attended = (numerator / denominator[..., None]).reshape(token_num, HQ * HEAD_WIDTH).astype(jnp.bfloat16)
    return (attended, highest + jnp.log(denominator))

def head_dot(output_gradient, attended):
    token_num = output_gradient.shape[0]
    joined = output_gradient.astype(jnp.float32) * attended.astype(jnp.float32)
    return lax.optimization_barrier(jnp.sum(joined.reshape(token_num, HQ, HEAD_WIDTH), axis=2))

def reference(queries, tile_ids, keys, values, patch_counts, output_gradient):
    blocks = TOKENS // TOK_DEV
    row_width = HQ * HEAD_WIDTH
    slot_total = IMAGE_TILES * CAP

    def block_step(totals, block_data):
        query_block, id_block, grad_block = block_data
        flat_slot = route_slots(id_block, IMAGE_TILES, CAP)
        index_map = dispatch_index(flat_slot, slot_total)
        query_rows = padded_take(query_block, index_map).reshape(IMAGE_TILES, CAP, row_width)
        part_out, part_max, part_total = tile_forward(query_rows, keys, values, patch_counts)
        attended, log_total = merge_partials(part_out.reshape(slot_total, row_width)[flat_slot], part_max.reshape(slot_total, HQ)[flat_slot], part_total.reshape(slot_total, HQ)[flat_slot])
        grad_dot = head_dot(grad_block, attended)
        grad_rows = padded_take(grad_block, index_map).reshape(IMAGE_TILES, CAP, row_width)
        total_rows = padded_take(log_total, index_map).reshape(IMAGE_TILES, CAP, HQ)
        dot_rows = padded_take(grad_dot, index_map).reshape(IMAGE_TILES, CAP, HQ)
        query_terms, key_terms, value_terms = tile_backward(query_rows, grad_rows, total_rows, dot_rows, keys, values, patch_counts)
        query_grad = lax.optimization_barrier(jnp.sum(query_terms.reshape(slot_total, row_width)[flat_slot], axis=1)).astype(jnp.bfloat16)
        return ((totals[0] + key_terms, totals[1] + value_terms), (attended, query_grad))
    zero_gradient = jnp.zeros((IMAGE_TILES, TILE_PATCH_ROWS, LOCAL_KV_HEADS * HEAD_WIDTH), jnp.float32)
    inputs = (queries.reshape(blocks, TOK_DEV, row_width), tile_ids.reshape(blocks, TOK_DEV, LIST), output_gradient.reshape(blocks, TOK_DEV, row_width))
    sums, stacked = lax.scan(block_step, (zero_gradient, zero_gradient), inputs)
    return (stacked[0].reshape(TOKENS, row_width), stacked[1].reshape(TOKENS, row_width), sums[0], sums[1])
```

```python
import functools
import math

import jax
import jax.numpy as jnp
from jax import lax
from jax.experimental import pallas as pl
from jax.experimental.pallas import tpu as pltpu
from jax.sharding import Mesh, PartitionSpec as P

HEAD_WIDTH = 128
GROUP = 8
CAP = 9
MAIN = 8
F32 = jnp.float32
BF16 = jnp.bfloat16
ROWS_LAST = (((1,), (1,)), ((), ()))


def token_slots(ids, tile_num):
    tokens = ids.shape[0]
    lane = lax.broadcasted_iota(jnp.int32, (tokens, 128), 1)
    chosen = jnp.where(ids == lane, 1.0, 0.0).T
    row = lax.broadcasted_iota(jnp.int32, (tokens, tokens), 0)
    column = lax.broadcasted_iota(jnp.int32, (tokens, tokens), 1)
    earlier = jnp.where(row < column, 1.0, 0.0).astype(BF16)
    before = jnp.dot(chosen.astype(BF16), earlier, preferred_element_type=F32)
    place = jnp.where(chosen > 0.0, before, -1.0).astype(BF16)
    slots = tile_num * CAP
    slot = lax.broadcasted_iota(jnp.int32, (slots, 128), 0)
    ninth = slot >= tile_num * MAIN
    tile = jnp.where(ninth, slot - tile_num * MAIN, slot // MAIN)
    spread = jnp.where(tile == lax.broadcasted_iota(jnp.int32, (slots, 128), 1), 1.0, 0.0)
    held = jnp.dot(spread.astype(BF16), place, preferred_element_type=F32)
    turn = jnp.where(ninth, MAIN, slot % MAIN).astype(F32)
    return jnp.where(held == turn, 1.0, 0.0)


def dispatch_kernel(ids_ref, query_ref, grad_ref, sent_ref, slots_ref, ninth_ref):
    tile_num = sent_ref.shape[0]

    @pl.when(pl.program_id(0) == 0)
    def _():
        slots_ref[...] = token_slots(ids_ref[...], tile_num).astype(BF16)

    for first, source in ((0, query_ref), (HEAD_WIDTH, grad_ref)):
        lanes = slice(first, first + HEAD_WIDTH)
        rows = jnp.dot(slots_ref[...], source[...], preferred_element_type=F32)
        heads = [rows[:, h * HEAD_WIDTH : (h + 1) * HEAD_WIDTH] for h in range(GROUP)]
        for h in range(GROUP):
            ninth_ref[pl.ds(h, tile_num, stride=GROUP), :] = heads[h][tile_num * MAIN :]
        for t in range(tile_num):
            parts = [head[t * MAIN : (t + 1) * MAIN] for head in heads]
            parts.append(ninth_ref[t * GROUP : (t + 1) * GROUP, :])
            sent_ref[t, :, lanes] = jnp.concatenate(parts, axis=0).astype(BF16)


def dispatch(tile_ids, queries, output_gradient, part, tile_num):
    tokens = queries.shape[0]
    width = GROUP * HEAD_WIDTH
    block = pl.BlockSpec((tokens, width), lambda i: (0, 2 * i + part))
    return pl.pallas_call(
        dispatch_kernel,
        grid=(2,),
        in_specs=[pl.BlockSpec((tokens, 1), lambda i: (0, 0)), block, block],
        out_specs=pl.BlockSpec((tile_num, CAP * GROUP, 2 * HEAD_WIDTH), lambda i: (i, 0, 0)),
        out_shape=jax.ShapeDtypeStruct((2 * tile_num, CAP * GROUP, 2 * HEAD_WIDTH), BF16),
        scratch_shapes=[
            pltpu.VMEM((tile_num * CAP, tokens), BF16),
            pltpu.VMEM((tile_num * GROUP, HEAD_WIDTH), F32),
        ],
        compiler_params=pltpu.CompilerParams(vmem_limit_bytes=24 * 2**20),
        cost_estimate=pl.CostEstimate(flops=2 * 10**8, bytes_accessed=3 * 10**6, transcendentals=0),
        name="dispatch",
    )(tile_ids, queries, output_gradient)


def combine_kernel(ids_ref, back_ref, *refs):
    attended_ref, query_grad_ref, slots_ref, ninth_ref = refs[-4:]
    tile_num = back_ref.shape[0]

    @pl.when(pl.program_id(0) == 0)
    def _():
        slots_ref[...] = token_slots(ids_ref[...], tile_num).T.astype(BF16)

    for t in range(tile_num):
        last = back_ref[t, MAIN * GROUP :, :].astype(F32)
        ninth_ref[0, t * GROUP : (t + 1) * GROUP, :] = last[:, :HEAD_WIDTH]
        ninth_ref[1, t * GROUP : (t + 1) * GROUP, :] = last[:, HEAD_WIDTH:]
    for h in range(GROUP):
        lanes = slice(h * HEAD_WIDTH, (h + 1) * HEAD_WIDTH)
        parts = [back_ref[t, h * MAIN : (h + 1) * MAIN, :].astype(F32) for t in range(tile_num)]
        main = jnp.concatenate(parts, axis=0)
        for side, target in ((0, attended_ref), (1, query_grad_ref)):
            ninth = ninth_ref[side, pl.ds(h, tile_num, stride=GROUP), :]
            half = main[:, side * HEAD_WIDTH : (side + 1) * HEAD_WIDTH]
            rows = jnp.concatenate([half, ninth], axis=0).astype(BF16)
            target[:, lanes] = jnp.dot(
                slots_ref[...], rows, preferred_element_type=F32
            ).astype(BF16)


def combine(tile_ids, back, part, earlier, shape):
    tokens = shape[0]
    tile_num = back.shape[0] // 2
    width = GROUP * HEAD_WIDTH
    block = pl.BlockSpec((tokens, width), lambda i: (0, 2 * i + part))
    whole = pl.BlockSpec(memory_space=pl.ANY)
    return pl.pallas_call(
        combine_kernel,
        grid=(2,),
        in_specs=[
            pl.BlockSpec((tokens, 1), lambda i: (0, 0)),
            pl.BlockSpec((tile_num, CAP * GROUP, 2 * HEAD_WIDTH), lambda i: (i, 0, 0)),
        ]
        + [whole] * len(earlier),
        out_specs=[block, block],
        out_shape=[jax.ShapeDtypeStruct(shape, BF16)] * 2,
        scratch_shapes=[
            pltpu.VMEM((tokens, tile_num * CAP), BF16),
            pltpu.VMEM((2, tile_num * GROUP, HEAD_WIDTH), F32),
        ],
        input_output_aliases={2: 0, 3: 1} if earlier else {},
        compiler_params=pltpu.CompilerParams(vmem_limit_bytes=24 * 2**20),
        cost_estimate=pl.CostEstimate(flops=2 * 10**8, bytes_accessed=3 * 10**6, transcendentals=0),
        name="combine",
    )(tile_ids, back, *earlier)


def attend_kernel(
    info, rows_ref, key_ref, value_ref, back_ref, grads_ref,
    query_s, grad_s, out_s, query_grad_s, key_fill, key_zero, value_ones,
    score_s, prob_s, slope_s, key_grad_s, value_grad_s, *, block_rows,
):
    count = info[1]
    device_num, slot_rows, _ = rows_ref.shape
    patches = key_ref.shape[1]
    width = HEAD_WIDTH
    inv_root = 1.0 / math.sqrt(width)
    to_power = math.log2(math.e) * inv_root

    live = lax.broadcasted_iota(jnp.int32, (patches, width), 0) < count
    key, value = key_ref[0].astype(F32), value_ref[0].astype(F32)
    key_fill[...] = jnp.where(live, key, key[0:1, :]).astype(BF16)
    key_zero[...] = jnp.where(live, key, 0.0).astype(BF16)
    value_ones[:, :width] = jnp.where(live, value, 0.0).astype(BF16)
    value_ones[:, width:] = jnp.where(live, 1.0, 0.0).astype(BF16)
    for i in range(0, device_num, 2):
        for first, target in ((0, query_s), (width, grad_s)):
            pair = [rows_ref[i + j, :, first : first + width].astype(F32) for j in range(2)]
            target[i * slot_rows : (i + 2) * slot_rows, :] = jnp.concatenate(pair, axis=0).astype(BF16)
    key_grad_s[...] = jnp.zeros_like(key_grad_s)
    value_grad_s[...] = jnp.zeros_like(value_grad_s)

    @pl.loop(0, query_s.shape[0] // block_rows)
    def _(step):
        here = pl.ds(pl.multiple_of(step * block_rows, block_rows), block_rows)
        query = query_s[here, :]
        score = lax.dot_general(query, key_fill[...], ROWS_LAST, preferred_element_type=F32)
        score_s[...] = score
        peak = jnp.max(score, axis=1, keepdims=True) * to_power
        prob_s[...] = jnp.exp2(score_s[...] * to_power - peak).astype(BF16)
        mixed = jnp.dot(prob_s[...], value_ones[...], preferred_element_type=F32)
        scale = 1.0 / mixed[:, width:]
        attended = (mixed[:, :width] * scale).astype(BF16).astype(F32)
        out_s[here, :] = attended
        grad = (grad_s[here, :].astype(F32) * scale).astype(BF16)
        grad_dot = jnp.sum(grad.astype(F32) * attended, axis=1, keepdims=True)
        prob_grad = lax.dot_general(
            grad, value_ones[:, :width], ROWS_LAST, preferred_element_type=F32
        )
        slope_s[...] = (prob_grad - grad_dot).astype(BF16) * prob_s[...]
        query_grad_s[here, :] = inv_root * jnp.dot(
            slope_s[...], key_zero[...], preferred_element_type=F32
        )
        grad_turned = grad.astype(F32).T.astype(BF16)
        query_turned = query.astype(F32).T.astype(BF16)
        value_grad_s[...] += jnp.dot(grad_turned, prob_s[...], preferred_element_type=F32)
        key_grad_s[...] += jnp.dot(query_turned, slope_s[...], preferred_element_type=F32)

    for i in range(device_num):
        own = slice(i * slot_rows, (i + 1) * slot_rows)
        back_ref[i, :, :width] = out_s[own, :].astype(BF16)
        back_ref[i, :, width:] = query_grad_s[own, :].astype(BF16)
    grads_ref[:, :width] = jnp.where(live, key_grad_s[...].T * inv_root, 0.0).astype(BF16)
    grads_ref[:, width:] = jnp.where(live, value_grad_s[...].T, 0.0).astype(BF16)


def attend(info, rows, keys, values):
    device_num, slot_rows, both = rows.shape
    patches = keys.shape[1]
    total = device_num * slot_rows
    width = HEAD_WIDTH
    block_rows = total // 3
    tile = pl.BlockSpec((1, patches, width), lambda i, info: (0, 0, info[0]))
    whole = pl.BlockSpec(rows.shape, lambda i, info: (0, 0, 0))
    return pl.pallas_call(
        functools.partial(attend_kernel, block_rows=block_rows),
        grid_spec=pltpu.PrefetchScalarGridSpec(
            num_scalar_prefetch=1,
            grid=(1,),
            in_specs=[whole, tile, tile],
            out_specs=[whole, pl.BlockSpec((patches, both), lambda i, info: (0, 0))],
            scratch_shapes=[
                pltpu.VMEM((total, width), BF16),
                pltpu.VMEM((total, width), BF16),
                pltpu.VMEM((total, width), F32),
                pltpu.VMEM((total, width), F32),
                pltpu.VMEM((patches, width), BF16),
                pltpu.VMEM((patches, width), BF16),
                pltpu.VMEM((patches, both), BF16),
                pltpu.VMEM((block_rows, patches), F32),
                pltpu.VMEM((block_rows, patches), BF16),
                pltpu.VMEM((block_rows, patches), BF16),
                pltpu.VMEM((width, patches), F32),
                pltpu.VMEM((width, patches), F32),
            ],
        ),
        out_shape=[
            jax.ShapeDtypeStruct(rows.shape, BF16),
            jax.ShapeDtypeStruct((patches, both), BF16),
        ],
        compiler_params=pltpu.CompilerParams(vmem_limit_bytes=40 * 2**20),
        cost_estimate=pl.CostEstimate(
            flops=12 * total * patches * width,
            bytes_accessed=4 * 10**6,
            transcendentals=total * patches,
        ),
        name="attend",
    )(info, rows, keys, values)


def local(queries, tile_ids, keys, values, patch_counts, output_gradient):
    tile_num = lax.axis_size("img")
    core = lax.axis_index("core")
    exchange = functools.partial(
        lax.all_to_all, axis_name=("core", "img"), split_axis=0, concat_axis=0, tiled=True
    )
    rows = [
        exchange(dispatch(tile_ids, queries, output_gradient, part, tile_num)) for part in range(2)
    ]
    outputs, sums = (), []
    for part in range(2):
        info = jnp.stack([2 * core + part, patch_counts[0]]).astype(jnp.int32)
        back, grads = attend(info, rows[part], keys, values)
        sums.append(lax.psum_scatter(grads, "z", scatter_dimension=0, tiled=True))
        outputs = combine(tile_ids, exchange(back), part, outputs, queries.shape)
    both = jnp.concatenate(sums, axis=1)
    half = both.shape[0] // 2
    mine = lax.dynamic_slice_in_dim(both, core * half, half, 0)
    theirs = lax.dynamic_slice_in_dim(both, (1 - core) * half, half, 0)
    other = lax.ppermute(theirs, "core", [(0, 1), (1, 0)])
    first = jnp.where(core == 0, mine, other).astype(F32)
    second = jnp.where(core == 0, other, mine).astype(F32)
    width = HEAD_WIDTH
    grads = [
        jnp.concatenate([side[:, a : a + width] for side in (first, second) for a in (b, b + 2 * width)], axis=1)[None]
        for b in (0, width)
    ]
    return (*outputs, *grads)


def solution(mesh):
    ctx, img = mesh.devices.shape
    fine = Mesh(mesh.devices.reshape(ctx // 2, 2, img), ("z", "core", "img"))
    rows = P(("z", "core", "img"), None)
    grads = P("img", ("z", "core"), None)
    tiles = P("img", None, None)
    return jax.shard_map(
        local,
        mesh=fine,
        in_specs=(rows, rows, tiles, tiles, P("img"), rows),
        out_specs=(rows, rows, grads, grads),
        check_vma=False,
    )
```

```python
import functools
import math

import jax
import jax.numpy as jnp
from jax import lax
from jax.experimental import pallas as pl
from jax.experimental.pallas import tpu as pltpu
from jax.sharding import Mesh, PartitionSpec as P

HEAD_WIDTH = 128
GROUP = 8
CAP = 9
MAIN = 8
F32 = jnp.float32
BF16 = jnp.bfloat16
ROWS_LAST = (((1,), (1,)), ((), ()))
LIMIT = 60 * 2**20
WAYS = 9


def token_slots(ids, tile_num):
    tokens = ids.shape[1]
    chosen = jnp.where(ids == lax.broadcasted_iota(jnp.int32, (128, tokens), 0), 1.0, 0.0)
    row = lax.broadcasted_iota(jnp.int32, (tokens, tokens), 0)
    column = lax.broadcasted_iota(jnp.int32, (tokens, tokens), 1)
    earlier = jnp.where(row < column, 1.0, 0.0).astype(BF16)
    before = jnp.dot(chosen.astype(BF16), earlier, preferred_element_type=F32)
    place = jnp.where(chosen > 0.0, before, -1.0).astype(BF16)
    slots = tile_num * CAP
    slot = lax.broadcasted_iota(jnp.int32, (slots, 128), 0)
    ninth = slot >= tile_num * MAIN
    tile = jnp.where(ninth, slot - tile_num * MAIN, slot // MAIN)
    spread = jnp.where(tile == lax.broadcasted_iota(jnp.int32, (slots, 128), 1), 1.0, 0.0)
    held = jnp.dot(spread.astype(BF16), place, preferred_element_type=F32)
    turn = jnp.where(ninth, MAIN, slot % MAIN).astype(F32)
    return jnp.where(held == turn, 1.0, 0.0)


def route_kernel(ids_ref, query_ref, grad_ref, sent_ref, slots_ref, turned_ref, ninth_ref):
    @pl.when(pl.program_id(0) == 0)
    def _():
        slots = token_slots(ids_ref[...], sent_ref.shape[0])
        slots_ref[...] = slots.astype(BF16)
        turned_ref[...] = slots.T.astype(BF16)

    dispatch_kernel(slots_ref, query_ref, grad_ref, sent_ref, ninth_ref)


def dispatch_kernel(slots_ref, query_ref, grad_ref, sent_ref, ninth_ref):
    tile_num = sent_ref.shape[0]
    for first, source in ((0, query_ref), (HEAD_WIDTH, grad_ref)):
        lanes = slice(first, first + HEAD_WIDTH)
        rows = jnp.dot(slots_ref[...], source[...], preferred_element_type=F32)
        heads = [rows[:, h * HEAD_WIDTH : (h + 1) * HEAD_WIDTH] for h in range(GROUP)]
        for h in range(GROUP):
            ninth_ref[pl.ds(h, tile_num, stride=GROUP), :] = heads[h][tile_num * MAIN :]
        for t in range(tile_num):
            parts = [head[t * MAIN : (t + 1) * MAIN] for head in heads]
            parts.append(ninth_ref[t * GROUP : (t + 1) * GROUP, :])
            sent_ref[t, :, lanes] = jnp.concatenate(parts, axis=0).astype(BF16)


def dispatch(routing, queries, output_gradient, part, tile_num):
    tokens = queries.shape[0]
    width = GROUP * HEAD_WIDTH
    block = pl.BlockSpec((tokens, width), lambda i: (0, 2 * i + part))
    fixed = lambda shape: pl.BlockSpec(shape, lambda i: (0, 0))
    out_specs = [pl.BlockSpec((tile_num, CAP * GROUP, 2 * HEAD_WIDTH), lambda i: (i, 0, 0))]
    out_shape = [jax.ShapeDtypeStruct((2 * tile_num, CAP * GROUP, 2 * HEAD_WIDTH), BF16)]
    if part == 0:
        for shape in ((tile_num * CAP, tokens), (tokens, tile_num * CAP)):
            out_specs.append(fixed(shape))
            out_shape.append(jax.ShapeDtypeStruct(shape, BF16))
    return pl.pallas_call(
        route_kernel if part == 0 else dispatch_kernel,
        grid=(2,),
        in_specs=[fixed(routing.shape), block, block],
        out_specs=out_specs,
        out_shape=out_shape,
        scratch_shapes=[pltpu.VMEM((tile_num * GROUP, HEAD_WIDTH), F32)],
        compiler_params=pltpu.CompilerParams(vmem_limit_bytes=LIMIT),
        cost_estimate=pl.CostEstimate(flops=10**9, bytes_accessed=3 * 10**6, transcendentals=0),
        name="dispatch",
    )(routing, queries, output_gradient)


def combine_kernel(turned_ref, back_ref, *refs):
    attended_ref, query_grad_ref, ninth_ref = refs[-3:]
    tile_num = back_ref.shape[0]
    for t in range(tile_num):
        last = back_ref[t, MAIN * GROUP :, :].astype(F32)
        ninth_ref[0, t * GROUP : (t + 1) * GROUP, :] = last[:, :HEAD_WIDTH]
        ninth_ref[1, t * GROUP : (t + 1) * GROUP, :] = last[:, HEAD_WIDTH:]
    for h in range(GROUP):
        lanes = slice(h * HEAD_WIDTH, (h + 1) * HEAD_WIDTH)
        parts = [back_ref[t, h * MAIN : (h + 1) * MAIN, :].astype(F32) for t in range(tile_num)]
        main = jnp.concatenate(parts, axis=0)
        for side, target in ((0, attended_ref), (1, query_grad_ref)):
            ninth = ninth_ref[side, pl.ds(h, tile_num, stride=GROUP), :]
            half = main[:, side * HEAD_WIDTH : (side + 1) * HEAD_WIDTH]
            rows = jnp.concatenate([half, ninth], axis=0).astype(BF16)
            target[:, lanes] = jnp.dot(
                turned_ref[...], rows, preferred_element_type=F32
            ).astype(BF16)


def combine(turned, back, part, earlier, shape):
    tokens = shape[0]
    tile_num = back.shape[0] // 2
    width = GROUP * HEAD_WIDTH
    block = pl.BlockSpec((tokens, width), lambda i: (0, 2 * i + part))
    whole = pl.BlockSpec(memory_space=pl.ANY)
    return pl.pallas_call(
        combine_kernel,
        grid=(2,),
        in_specs=[
            pl.BlockSpec(turned.shape, lambda i: (0, 0)),
            pl.BlockSpec((tile_num, CAP * GROUP, 2 * HEAD_WIDTH), lambda i: (i, 0, 0)),
        ]
        + [whole] * len(earlier),
        out_specs=[block, block],
        out_shape=[jax.ShapeDtypeStruct(shape, BF16)] * 2,
        scratch_shapes=[pltpu.VMEM((2, tile_num * GROUP, HEAD_WIDTH), F32)],
        input_output_aliases={2: 0, 3: 1} if earlier else {},
        compiler_params=pltpu.CompilerParams(vmem_limit_bytes=LIMIT),
        cost_estimate=pl.CostEstimate(flops=10**9, bytes_accessed=3 * 10**6, transcendentals=0),
        name="combine",
    )(turned, back, *earlier)


def attend_kernel(info, rows_ref, key_ref, value_ref, back_ref, *refs, ways):
    scratch = refs[-(10 + 3 * ways) :]
    shares = refs[: -len(scratch)]
    query_s, grad_s, out_s, query_grad_s, key_fill, key_zero, value_ones = scratch[:7]
    key_grad_s, value_grad_s, grads_s = scratch[7:10]
    score_s, prob_s, slope_s = (scratch[10 + i * ways : 10 + (i + 1) * ways] for i in range(3))
    device_num, slot_rows, _ = rows_ref.shape
    patches = key_ref.shape[1]
    width = HEAD_WIDTH
    block_rows = query_s.shape[0] // ways
    inv_root = 1.0 / math.sqrt(width)
    to_power = math.log2(math.e) * inv_root

    live = lax.broadcasted_iota(jnp.int32, (patches, width), 0) < info[2]
    key, value = key_ref[0].astype(F32), value_ref[0].astype(F32)
    key_fill[...] = jnp.where(live, key, key[0:1, :]).astype(BF16)
    key_zero[...] = jnp.where(live, key, 0.0).astype(BF16)
    value_ones[:, :width] = jnp.where(live, value, 0.0).astype(BF16)
    value_ones[:, width:] = jnp.where(live, 1.0, 0.0).astype(BF16)
    for i in range(0, device_num, 2):
        for first, target in ((0, query_s), (width, grad_s)):
            pair = [rows_ref[i + j, :, first : first + width].astype(F32) for j in range(2)]
            target[i * slot_rows : (i + 2) * slot_rows, :] = jnp.concatenate(pair, axis=0).astype(BF16)
    key_grad_s[...] = jnp.zeros_like(key_grad_s)
    value_grad_s[...] = jnp.zeros_like(value_grad_s)

    here = [slice(w * block_rows, (w + 1) * block_rows) for w in range(ways)]
    peak, grad, grad_dot = {}, {}, {}

    def scores(w):
        score = lax.dot_general(
            query_s[here[w], :], key_fill[...], ROWS_LAST, preferred_element_type=F32
        )
        score_s[w][...] = score
        peak[w] = jnp.max(score, axis=1, keepdims=True) * to_power

    def weights(w):
        prob_s[w][...] = jnp.exp2(score_s[w][...] * to_power - peak[w]).astype(BF16)

    def output(w):
        mixed = jnp.dot(prob_s[w][...], value_ones[...], preferred_element_type=F32)
        scale = 1.0 / mixed[:, width:]
        attended = (mixed[:, :width] * scale).astype(BF16).astype(F32)
        out_s[here[w], :] = attended
        grad[w] = (grad_s[here[w], :].astype(F32) * scale).astype(BF16)
        grad_dot[w] = jnp.sum(grad[w].astype(F32) * attended, axis=1, keepdims=True)

    def slopes(w):
        prob_grad = lax.dot_general(
            grad[w], value_ones[:, :width], ROWS_LAST, preferred_element_type=F32
        )
        slope_s[w][...] = (prob_grad - grad_dot[w]).astype(BF16) * prob_s[w][...]

    def value_term(w):
        turned = grad[w].astype(F32).T.astype(BF16)
        value_grad_s[...] += jnp.dot(turned, prob_s[w][...], preferred_element_type=F32)

    def query_term(w):
        query_grad_s[here[w], :] = inv_root * jnp.dot(
            slope_s[w][...], key_zero[...], preferred_element_type=F32
        )

    def key_term(w):
        turned = query_s[here[w], :].astype(F32).T.astype(BF16)
        key_grad_s[...] += jnp.dot(turned, slope_s[w][...], preferred_element_type=F32)

    steps = (scores, weights, output, slopes, value_term, query_term, key_term)
    for now in range(len(steps) + ways - 1):
        for w in range(ways):
            if 0 <= now - w < len(steps):
                steps[now - w](w)

    for i in range(device_num):
        own = slice(i * slot_rows, (i + 1) * slot_rows)
        back_ref[i, :, :width] = out_s[own, :].astype(BF16)
        back_ref[i, :, width:] = query_grad_s[own, :].astype(BF16)
    live = lax.broadcasted_iota(jnp.int32, (width, patches), 1) < info[2]
    key_grad_s[...] = jnp.where(live, key_grad_s[...] * inv_root, 0.0)
    value_grad_s[...] = jnp.where(live, value_grad_s[...], 0.0)
    grads_s[:, :width] = key_grad_s[...].T
    grads_s[:, width:] = value_grad_s[...].T
    for i, share in enumerate(shares):
        part = lax.rem(info[1] + i, len(shares))
        size = share.shape[0]
        share[...] = grads_s[pl.ds(pl.multiple_of(part * size, size), size), :].astype(BF16)


def attend(info, rows, keys, values, part, share_num):
    device_num, slot_rows, both = rows.shape
    patches = keys.shape[1]
    total = device_num * slot_rows
    width = HEAD_WIDTH
    share = patches // share_num
    ways = WAYS
    block_rows = total // ways
    tile = pl.BlockSpec((1, patches, width), lambda i, info: (0, 0, 2 * info[0] + part))
    whole = pl.BlockSpec(rows.shape, lambda i, info: (0, 0, 0))
    return pl.pallas_call(
        functools.partial(attend_kernel, ways=ways),
        grid_spec=pltpu.PrefetchScalarGridSpec(
            num_scalar_prefetch=1,
            grid=(1,),
            in_specs=[whole, tile, tile],
            out_specs=[whole] + [pl.BlockSpec((share, both), lambda i, info: (0, 0))] * share_num,
            scratch_shapes=[
                pltpu.VMEM((total, width), BF16),
                pltpu.VMEM((total, width), BF16),
                pltpu.VMEM((total, width), F32),
                pltpu.VMEM((total, width), F32),
                pltpu.VMEM((patches, width), BF16),
                pltpu.VMEM((patches, width), BF16),
                pltpu.VMEM((patches, both), BF16),
                pltpu.VMEM((width, patches), F32),
                pltpu.VMEM((width, patches), F32),
                pltpu.VMEM((patches, both), F32),
            ]
            + [pltpu.VMEM((block_rows, patches), F32)] * ways
            + [pltpu.VMEM((block_rows, patches), BF16)] * (2 * ways),
        ),
        out_shape=[jax.ShapeDtypeStruct(rows.shape, BF16)]
        + [jax.ShapeDtypeStruct((share, both), BF16)] * share_num,
        compiler_params=pltpu.CompilerParams(vmem_limit_bytes=LIMIT),
        cost_estimate=pl.CostEstimate(
            flops=60 * total * patches * width,
            bytes_accessed=4 * 10**6,
            transcendentals=total * patches,
        ),
        name="attend",
    )(info, rows, keys, values)


def add_kernel(info, *refs):
    shares, (mine_ref, theirs_ref) = refs[:-2], refs[-2:]
    half, both = mine_ref.shape[0], shares[0].shape[1]
    for part in range(2):
        of_part = shares[part * len(shares) // 2 : (part + 1) * len(shares) // 2]
        lanes = slice(part * both, (part + 1) * both)
        for target, core in ((mine_ref, info[0]), (theirs_ref, 1 - info[0])):
            rows = pl.ds(pl.multiple_of(core * half, half), half)
            total = sum(share[rows, :].astype(F32) for share in of_part)
            target[:, lanes] = total.astype(target.dtype)


def add_shares(info, shares):
    rows, both = shares[0].shape
    half = rows // 2
    return pl.pallas_call(
        add_kernel,
        grid_spec=pltpu.PrefetchScalarGridSpec(
            num_scalar_prefetch=1,
            grid=(1,),
            in_specs=[pl.BlockSpec((rows, both), lambda i, info: (0, 0))] * len(shares),
            out_specs=[pl.BlockSpec((half, 2 * both), lambda i, info: (0, 0))] * 2,
        ),
        out_shape=[
            jax.ShapeDtypeStruct((half, 2 * both), F32),
            jax.ShapeDtypeStruct((half, 2 * both), BF16),
        ],
        compiler_params=pltpu.CompilerParams(vmem_limit_bytes=LIMIT),
        cost_estimate=pl.CostEstimate(flops=10**8, bytes_accessed=10**6, transcendentals=0),
        name="add_shares",
    )(info, *shares)


def local(queries, tile_ids, keys, values, patch_counts, output_gradient):
    tile_num = lax.axis_size("img")
    depth = lax.axis_size("z")
    info = jnp.stack([lax.axis_index("core"), lax.axis_index("z"), patch_counts[0]]).astype(jnp.int32)
    exchange = functools.partial(
        lax.all_to_all, axis_name=("core", "img"), split_axis=0, concat_axis=0, tiled=True
    )
    ids = tile_ids.reshape(1, -1)
    sent, slots, turned = dispatch(ids, queries, output_gradient, 0, tile_num)
    (later,) = dispatch(slots, queries, output_gradient, 1, tile_num)
    rows, later = lax.optimization_barrier((exchange(sent), later))
    rows = [rows, exchange(later)]
    along_z = lambda shares: [
        lax.ppermute(shares[s], "z", [(i, (i + s) % depth) for i in range(depth)])
        for s in range(1, depth)
    ]
    back, own, *shares = attend(info, rows[0], keys, values, 0, depth)
    sums = [own, *along_z([own, *shares])]
    first_back = exchange(back)
    back, own, *shares = attend(info, rows[1], keys, values, 1, depth)
    back, sums = lax.optimization_barrier((back, sums))
    second_back = exchange(back)
    outputs = combine(turned, first_back, 0, (), queries.shape)
    sums = sums + [own, *along_z([own, *shares])]
    sums, outputs = lax.optimization_barrier((sums, outputs))
    mine, given = add_shares(info, sums)
    other = lax.ppermute(given, "core", [(0, 1), (1, 0)]).astype(F32)
    outputs = combine(turned, second_back, 1, outputs, queries.shape)
    core = lax.axis_index("core")
    sides = (jnp.where(core == 0, mine, other), jnp.where(core == 0, other, mine))
    width = HEAD_WIDTH
    grads = [
        jnp.concatenate(
            [side[:, a : a + width] for side in sides for a in (first, first + 2 * width)], axis=1
        )[None]
        for first in (0, width)
    ]
    return (*outputs, *grads)


def solution(mesh):
    ctx, img = mesh.devices.shape
    fine = Mesh(mesh.devices.reshape(ctx // 2, 2, img), ("z", "core", "img"))
    rows = P(("z", "core", "img"), None)
    grads = P("img", ("z", "core"), None)
    tiles = P("img", None, None)
    return jax.shard_map(
        local,
        mesh=fine,
        in_specs=(rows, rows, tiles, tiles, P("img"), rows),
        out_specs=(rows, rows, grads, grads),
        check_vma=False,
    )
```

```python
import functools
import math

import jax
import jax.numpy as jnp
from jax import lax
from jax.experimental import pallas as pl
from jax.experimental.pallas import tpu as pltpu
from jax.sharding import Mesh, PartitionSpec as P

HEAD_WIDTH = 128
GROUP = 8
CAP = 9
MAIN = 8
F32 = jnp.float32
BF16 = jnp.bfloat16
ROWS_LAST = (((1,), (1,)), ((), ()))
LIMIT = 60 * 2**20
SMALL = 16 * 2**20
ATTEND_LIMITS = (32 * 2**20, 56 * 2**20)
WAYS = 9
TURNS = (3, 5, 5)


def token_slots(ids, tile_num):
    tokens = ids.shape[1]
    chosen = jnp.where(ids == lax.broadcasted_iota(jnp.int32, (128, tokens), 0), 1.0, 0.0)
    row = lax.broadcasted_iota(jnp.int32, (tokens, tokens), 0)
    column = lax.broadcasted_iota(jnp.int32, (tokens, tokens), 1)
    earlier = jnp.where(row < column, 1.0, 0.0).astype(BF16)
    before = jnp.dot(chosen.astype(BF16), earlier, preferred_element_type=F32)
    place = jnp.where(chosen > 0.0, before, -1.0).astype(BF16)
    slots = tile_num * CAP
    slot = lax.broadcasted_iota(jnp.int32, (slots, 128), 0)
    ninth = slot >= tile_num * MAIN
    tile = jnp.where(ninth, slot - tile_num * MAIN, slot // MAIN)
    spread = jnp.where(tile == lax.broadcasted_iota(jnp.int32, (slots, 128), 1), 1.0, 0.0)
    held = jnp.dot(spread.astype(BF16), place, preferred_element_type=F32)
    turn = jnp.where(ninth, MAIN, slot % MAIN).astype(F32)
    return jnp.where(held == turn, 1.0, 0.0)


def route_kernel(ids_ref, query_ref, grad_ref, sent_ref, slots_ref, turned_ref, ninth_ref):
    @pl.when(pl.program_id(0) == 0)
    def _():
        slots = token_slots(ids_ref[...], sent_ref.shape[0])
        slots_ref[...] = slots.astype(BF16)
        turned_ref[...] = slots.T.astype(BF16)

    dispatch_kernel(slots_ref, query_ref, grad_ref, sent_ref, ninth_ref)


def dispatch_kernel(slots_ref, query_ref, grad_ref, sent_ref, ninth_ref):
    tile_num = sent_ref.shape[0]
    for first, source in ((0, query_ref), (HEAD_WIDTH, grad_ref)):
        lanes = slice(first, first + HEAD_WIDTH)
        rows = jnp.dot(slots_ref[...], source[...], preferred_element_type=F32)
        heads = [rows[:, h * HEAD_WIDTH : (h + 1) * HEAD_WIDTH] for h in range(GROUP)]
        for h in range(GROUP):
            ninth_ref[pl.ds(h, tile_num, stride=GROUP), :] = heads[h][tile_num * MAIN :]
        for t in range(tile_num):
            parts = [head[t * MAIN : (t + 1) * MAIN] for head in heads]
            parts.append(ninth_ref[t * GROUP : (t + 1) * GROUP, :])
            sent_ref[t, :, lanes] = jnp.concatenate(parts, axis=0).astype(BF16)


def dispatch(routing, queries, output_gradient, part, tile_num):
    tokens = queries.shape[0]
    width = GROUP * HEAD_WIDTH
    block = pl.BlockSpec((tokens, width), lambda i: (0, 2 * i + part))
    fixed = lambda shape: pl.BlockSpec(shape, lambda i: (0, 0))
    out_specs = [pl.BlockSpec((tile_num, CAP * GROUP, 2 * HEAD_WIDTH), lambda i: (i, 0, 0))]
    out_shape = [jax.ShapeDtypeStruct((2 * tile_num, CAP * GROUP, 2 * HEAD_WIDTH), BF16)]
    if part == 0:
        for shape in ((tile_num * CAP, tokens), (tokens, tile_num * CAP)):
            out_specs.append(fixed(shape))
            out_shape.append(jax.ShapeDtypeStruct(shape, BF16))
    return pl.pallas_call(
        route_kernel if part == 0 else dispatch_kernel,
        grid=(2,),
        in_specs=[fixed(routing.shape), block, block],
        out_specs=out_specs,
        out_shape=out_shape,
        scratch_shapes=[pltpu.VMEM((tile_num * GROUP, HEAD_WIDTH), F32)],
        compiler_params=pltpu.CompilerParams(vmem_limit_bytes=LIMIT),
        cost_estimate=pl.CostEstimate(flops=10**9, bytes_accessed=3 * 10**6, transcendentals=0),
        name="dispatch",
    )(routing, queries, output_gradient)


def combine_kernel(turned_ref, back_ref, *refs):
    attended_ref, query_grad_ref, ninth_ref = refs[-3:]
    tile_num = back_ref.shape[0]
    for t in range(tile_num):
        last = back_ref[t, MAIN * GROUP :, :].astype(F32)
        ninth_ref[0, t * GROUP : (t + 1) * GROUP, :] = last[:, :HEAD_WIDTH]
        ninth_ref[1, t * GROUP : (t + 1) * GROUP, :] = last[:, HEAD_WIDTH:]
    for h in range(GROUP):
        lanes = slice(h * HEAD_WIDTH, (h + 1) * HEAD_WIDTH)
        parts = [back_ref[t, h * MAIN : (h + 1) * MAIN, :].astype(F32) for t in range(tile_num)]
        main = jnp.concatenate(parts, axis=0)
        for side, target in ((0, attended_ref), (1, query_grad_ref)):
            ninth = ninth_ref[side, pl.ds(h, tile_num, stride=GROUP), :]
            half = main[:, side * HEAD_WIDTH : (side + 1) * HEAD_WIDTH]
            rows = jnp.concatenate([half, ninth], axis=0).astype(BF16)
            target[:, lanes] = jnp.dot(
                turned_ref[...], rows, preferred_element_type=F32
            ).astype(BF16)


def combine(turned, back, part, earlier, shape):
    tokens = shape[0]
    tile_num = back.shape[0] // 2
    width = GROUP * HEAD_WIDTH
    block = pl.BlockSpec((tokens, width), lambda i: (0, 2 * i + part))
    whole = pl.BlockSpec(memory_space=pl.ANY)
    return pl.pallas_call(
        combine_kernel,
        grid=(2,),
        in_specs=[
            pl.BlockSpec(turned.shape, lambda i: (0, 0)),
            pl.BlockSpec((tile_num, CAP * GROUP, 2 * HEAD_WIDTH), lambda i: (i, 0, 0)),
        ]
        + [whole] * len(earlier),
        out_specs=[block, block],
        out_shape=[jax.ShapeDtypeStruct(shape, BF16)] * 2,
        scratch_shapes=[pltpu.VMEM((2, tile_num * GROUP, HEAD_WIDTH), F32)],
        input_output_aliases={2: 0, 3: 1} if earlier else {},
        compiler_params=pltpu.CompilerParams(vmem_limit_bytes=SMALL),
        cost_estimate=pl.CostEstimate(flops=10**6, bytes_accessed=10**5, transcendentals=0),
        name="combine",
    )(turned, back, *earlier)


def attend_kernel(info, rows_ref, key_ref, value_ref, back_ref, *refs, ways, depth):
    scratch = refs[-(10 + sum(TURNS)) :]
    shares = refs[: -len(scratch)]
    query_s, grad_s, out_s, query_grad_s, key_fill, key_zero, value_ones = scratch[:7]
    key_grad_s, value_grad_s, grads_s = scratch[7:10]
    buffers = list(scratch[10:])
    turns = [[buffers.pop(0) for _ in range(turn)] for turn in TURNS]
    score_s, prob_s, slope_s = ([turn[w % len(turn)] for w in range(ways)] for turn in turns)
    device_num, slot_rows, _ = rows_ref.shape
    patches = key_ref.shape[1]
    width = HEAD_WIDTH
    block_rows = query_s.shape[0] // ways
    inv_root = 1.0 / math.sqrt(width)
    to_power = math.log2(math.e) * inv_root

    live = lax.broadcasted_iota(jnp.int32, (patches, width), 0) < info[2]
    key, value = key_ref[0].astype(F32), value_ref[0].astype(F32)
    key_fill[...] = jnp.where(live, key, key[0:1, :]).astype(BF16)
    key_zero[...] = jnp.where(live, key, 0.0).astype(BF16)
    value_ones[:, :width] = jnp.where(live, value, 0.0).astype(BF16)
    value_ones[:, width:] = jnp.where(live, 1.0, 0.0).astype(BF16)
    for i in range(0, device_num, 2):
        for first, target in ((0, query_s), (width, grad_s)):
            pair = [rows_ref[i + j, :, first : first + width].astype(F32) for j in range(2)]
            target[i * slot_rows : (i + 2) * slot_rows, :] = jnp.concatenate(pair, axis=0).astype(BF16)
    key_grad_s[...] = jnp.zeros_like(key_grad_s)
    value_grad_s[...] = jnp.zeros_like(value_grad_s)

    here = [slice(w * block_rows, (w + 1) * block_rows) for w in range(ways)]
    peak, grad, grad_dot = {}, {}, {}

    def scores(w):
        score = lax.dot_general(
            query_s[here[w], :], key_fill[...], ROWS_LAST, preferred_element_type=F32
        )
        score_s[w][...] = score
        peak[w] = jnp.max(score, axis=1, keepdims=True) * to_power

    def weights(w):
        prob_s[w][...] = jnp.exp2(score_s[w][...] * to_power - peak[w]).astype(BF16)

    def output(w):
        mixed = jnp.dot(prob_s[w][...], value_ones[...], preferred_element_type=F32)
        scale = 1.0 / mixed[:, width:]
        attended = (mixed[:, :width] * scale).astype(BF16).astype(F32)
        out_s[here[w], :] = attended
        grad[w] = (grad_s[here[w], :].astype(F32) * scale).astype(BF16)
        grad_dot[w] = jnp.sum(grad[w].astype(F32) * attended, axis=1, keepdims=True)

    def slopes(w):
        prob_grad = lax.dot_general(
            grad[w], value_ones[:, :width], ROWS_LAST, preferred_element_type=F32
        )
        slope_s[w][...] = (prob_grad - grad_dot[w]).astype(BF16) * prob_s[w][...]

    def value_term(w):
        turned = grad[w].astype(F32).T.astype(BF16)
        value_grad_s[...] += jnp.dot(turned, prob_s[w][...], preferred_element_type=F32)

    def query_term(w):
        query_grad_s[here[w], :] = inv_root * jnp.dot(
            slope_s[w][...], key_zero[...], preferred_element_type=F32
        )

    def key_term(w):
        turned = query_s[here[w], :].astype(F32).T.astype(BF16)
        key_grad_s[...] += jnp.dot(turned, slope_s[w][...], preferred_element_type=F32)

    steps = (scores, weights, output, slopes, value_term, query_term, key_term)
    for now in range(len(steps) + ways - 1):
        for w in range(ways):
            if 0 <= now - w < len(steps):
                steps[now - w](w)

    for i in range(device_num):
        own = slice(i * slot_rows, (i + 1) * slot_rows)
        back_ref[i, :, :width] = out_s[own, :].astype(BF16)
        back_ref[i, :, width:] = query_grad_s[own, :].astype(BF16)
    live = lax.broadcasted_iota(jnp.int32, (width, patches), 1) < info[2]
    grads_s[:, :width] = jnp.where(live, key_grad_s[...] * inv_root, 0.0).T
    grads_s[:, width:] = jnp.where(live, value_grad_s[...], 0.0).T
    for i, share in enumerate(shares):
        size = share.shape[0]
        split = len(shares) // depth
        place = lax.rem(info[1] + i // split, depth) * split
        if split == 2:
            place = place + (info[0] if i % 2 == 0 else 1 - info[0])
        share[...] = grads_s[pl.ds(pl.multiple_of(place * size, size), size), :].astype(BF16)


def attend(info, rows, keys, values, depth, split):
    device_num, slot_rows, both = rows.shape
    patches = keys.shape[1]
    share_num = depth * split
    total = device_num * slot_rows
    width = HEAD_WIDTH
    share = patches // share_num
    ways = WAYS
    block_rows = total // ways
    tile = pl.BlockSpec((1, patches, width), lambda i, info: (0, 0, 0))
    whole = pl.BlockSpec(rows.shape, lambda i, info: (0, 0, 0))
    return pl.pallas_call(
        functools.partial(attend_kernel, ways=ways, depth=depth),
        grid_spec=pltpu.PrefetchScalarGridSpec(
            num_scalar_prefetch=1,
            grid=(1,),
            in_specs=[whole, tile, tile],
            out_specs=[whole] + [pl.BlockSpec((share, both), lambda i, info: (0, 0))] * share_num,
            scratch_shapes=[
                pltpu.VMEM((total, width), BF16),
                pltpu.VMEM((total, width), BF16),
                pltpu.VMEM((total, width), F32),
                pltpu.VMEM((total, width), F32),
                pltpu.VMEM((patches, width), BF16),
                pltpu.VMEM((patches, width), BF16),
                pltpu.VMEM((patches, both), BF16),
                pltpu.VMEM((width, patches), F32),
                pltpu.VMEM((width, patches), F32),
                pltpu.VMEM((patches, both), F32),
            ]
            + [pltpu.VMEM((block_rows, patches), F32)] * TURNS[0]
            + [pltpu.VMEM((block_rows, patches), BF16)] * (TURNS[1] + TURNS[2]),
        ),
        out_shape=[jax.ShapeDtypeStruct(rows.shape, BF16)]
        + [jax.ShapeDtypeStruct((share, both), BF16)] * share_num,
        compiler_params=pltpu.CompilerParams(vmem_limit_bytes=ATTEND_LIMITS[split - 1]),
        cost_estimate=pl.CostEstimate(
            flops=60 * total * patches * width,
            bytes_accessed=4 * 10**6,
            transcendentals=total * patches,
        ),
        name="attend",
    )(info, rows, keys, values)


def add_kernel(info, *refs):
    shares, (mine_ref, theirs_ref) = refs[:-2], refs[-2:]
    half = mine_ref.shape[0]
    for target, core in ((mine_ref, info[0]), (theirs_ref, 1 - info[0])):
        rows = pl.ds(pl.multiple_of(core * half, half), half)
        target[...] = sum(share[rows, :].astype(F32) for share in shares).astype(target.dtype)


def add_shares(info, shares):
    rows, both = shares[0].shape
    half = rows // 2
    fixed = lambda size: pl.BlockSpec((size, both), lambda i, info: (0, 0))
    return pl.pallas_call(
        add_kernel,
        grid_spec=pltpu.PrefetchScalarGridSpec(
            num_scalar_prefetch=1,
            grid=(1,),
            in_specs=[fixed(rows)] * len(shares),
            out_specs=[fixed(half)] * 2,
        ),
        out_shape=[jax.ShapeDtypeStruct((half, both), dtype) for dtype in (F32, BF16)],
        compiler_params=pltpu.CompilerParams(vmem_limit_bytes=SMALL),
        cost_estimate=pl.CostEstimate(flops=10**6, bytes_accessed=10**5, transcendentals=0),
        name="add_shares",
    )(info, *shares)


def place_kernel(info, *refs):
    (mine, other, *shares), (key_ref, value_ref) = refs[:-2], refs[-2:]
    width = HEAD_WIDTH
    parts = [(mine[...], other[...].astype(F32))]
    parts.append([sum(share[...].astype(F32) for share in shares[i::2]) for i in range(2)])
    for part, (own, theirs) in enumerate(parts):
        for core in range(2):
            chosen = jnp.where(info[0] == core, own, theirs)
            group = 2 * core + part
            for first, target in ((0, key_ref), (width, value_ref)):
                target[0, :, group * width : (group + 1) * width] = chosen[:, first : first + width]


def place(info, mine, other, shares):
    rows, both = mine.shape
    out = (1, rows, 2 * both)
    return pl.pallas_call(
        place_kernel,
        grid_spec=pltpu.PrefetchScalarGridSpec(
            num_scalar_prefetch=1,
            grid=(1,),
            in_specs=[pl.BlockSpec((rows, both), lambda i, info: (0, 0))] * (2 + len(shares)),
            out_specs=[pl.BlockSpec(out, lambda i, info: (0, 0, 0))] * 2,
        ),
        out_shape=[jax.ShapeDtypeStruct(out, F32)] * 2,
        compiler_params=pltpu.CompilerParams(vmem_limit_bytes=SMALL),
        cost_estimate=pl.CostEstimate(flops=10**6, bytes_accessed=10**5, transcendentals=0),
        name="place",
    )(info, mine, other, *shares)


def local(queries, tile_ids, keys, values, patch_counts, output_gradient):
    tile_num = lax.axis_size("img")
    depth = lax.axis_size("z")
    info = jnp.stack([lax.axis_index("core"), lax.axis_index("z"), patch_counts[0]]).astype(jnp.int32)
    exchange = functools.partial(
        lax.all_to_all, axis_name=("core", "img"), split_axis=0, concat_axis=0, tiled=True
    )
    ids = tile_ids.reshape(1, -1)
    sent, slots, turned = dispatch(ids, queries, output_gradient, 0, tile_num)
    (later,) = dispatch(slots, queries, output_gradient, 1, tile_num)
    first = 2 * lax.axis_index("core") * HEAD_WIDTH
    tiles = [
        [lax.dynamic_slice_in_dim(a, first + part * HEAD_WIDTH, HEAD_WIDTH, 2) for a in (keys, values)]
        for part in range(2)
    ]
    rows, later, tiles = lax.optimization_barrier((exchange(sent), later, tiles))
    rows = [rows, exchange(later)]
    back, *shares = attend(info, rows[0], *tiles[0], depth, 1)
    first_back = exchange(back)
    shares, rows = lax.optimization_barrier((shares, rows))
    for i in range(1, depth):
        shares[i] = lax.ppermute(shares[i], "z", [(z, (z + i) % depth) for z in range(depth)])
    back, *later = attend(info, rows[1], *tiles[1], depth, 2)
    back, shares = lax.optimization_barrier((back, shares))
    second_back = exchange(back)
    for i in range(1, 2 * depth):
        to = lambda z, core: ((z + i // 2) % depth) * 2 + (core + i) % 2
        pairs = [(2 * z + core, to(z, core)) for z in range(depth) for core in range(2)]
        later[i] = lax.ppermute(later[i], ("z", "core"), pairs)
    mine, given = add_shares(info, shares)
    other = lax.ppermute(given, "core", [(0, 1), (1, 0)])
    outputs = combine(turned, first_back, 0, (), queries.shape)
    grads = place(info, mine, other, later)
    outputs = combine(turned, second_back, 1, outputs, queries.shape)
    return (*outputs, *grads)


def solution(mesh):
    ctx, img = mesh.devices.shape
    fine = Mesh(mesh.devices.reshape(ctx // 2, 2, img), ("z", "core", "img"))
    rows = P(("z", "core", "img"), None)
    grads = P("img", ("z", "core"), None)
    tiles = P("img", None, None)
    return jax.shard_map(
        local,
        mesh=fine,
        in_specs=(rows, rows, tiles, tiles, P("img"), rows),
        out_specs=(rows, rows, grads, grads),
        check_vma=False,
    )
```

```python
import functools
import math

import jax
import jax.numpy as jnp
from jax import lax
from jax.experimental import pallas as pl
from jax.experimental.pallas import tpu as pltpu
from jax.sharding import Mesh, PartitionSpec as P

HEAD_WIDTH = 128
GROUP = 8
CAP = 9
MAIN = 8
F32 = jnp.float32
BF16 = jnp.bfloat16
ROWS_LAST = (((1,), (1,)), ((), ()))
LIMIT = 60 * 2**20
SMALL = 16 * 2**20
ATTEND_LIMITS = (32 * 2**20, 56 * 2**20)
WAYS = 9
TURNS = (3, 5, 5)


def token_slots(ids, tile_num):
    tokens = ids.shape[1]
    chosen = jnp.where(ids == lax.broadcasted_iota(jnp.int32, (128, tokens), 0), 1.0, 0.0)
    row = lax.broadcasted_iota(jnp.int32, (tokens, tokens), 0)
    column = lax.broadcasted_iota(jnp.int32, (tokens, tokens), 1)
    earlier = jnp.where(row < column, 1.0, 0.0).astype(BF16)
    before = jnp.dot(chosen.astype(BF16), earlier, preferred_element_type=F32)
    place = jnp.where(chosen > 0.0, before, -1.0).astype(BF16)
    slots = tile_num * CAP
    slot = lax.broadcasted_iota(jnp.int32, (slots, 128), 0)
    ninth = slot >= tile_num * MAIN
    tile = jnp.where(ninth, slot - tile_num * MAIN, slot // MAIN)
    spread = jnp.where(tile == lax.broadcasted_iota(jnp.int32, (slots, 128), 1), 1.0, 0.0)
    held = jnp.dot(spread.astype(BF16), place, preferred_element_type=F32)
    turn = jnp.where(ninth, MAIN, slot % MAIN).astype(F32)
    return jnp.where(held == turn, 1.0, 0.0)


def route_kernel(ids_ref, query_ref, grad_ref, sent_ref, slots_ref, turned_ref, ninth_ref):
    @pl.when(pl.program_id(0) == 0)
    def _():
        slots = token_slots(ids_ref[...], sent_ref.shape[0])
        slots_ref[...] = slots.astype(BF16)
        turned_ref[...] = slots.T.astype(BF16)

    dispatch_kernel(slots_ref, query_ref, grad_ref, sent_ref, ninth_ref)


def dispatch_kernel(slots_ref, query_ref, grad_ref, sent_ref, ninth_ref):
    tile_num = sent_ref.shape[0]
    for first, source in ((0, query_ref), (HEAD_WIDTH, grad_ref)):
        lanes = slice(first, first + HEAD_WIDTH)
        rows = jnp.dot(slots_ref[...], source[...], preferred_element_type=F32)
        heads = [rows[:, h * HEAD_WIDTH : (h + 1) * HEAD_WIDTH] for h in range(GROUP)]
        for h in range(GROUP):
            ninth_ref[pl.ds(h, tile_num, stride=GROUP), :] = heads[h][tile_num * MAIN :]
        for t in range(tile_num):
            parts = [head[t * MAIN : (t + 1) * MAIN] for head in heads]
            parts.append(ninth_ref[t * GROUP : (t + 1) * GROUP, :])
            sent_ref[t, :, lanes] = jnp.concatenate(parts, axis=0).astype(BF16)


def dispatch(routing, queries, output_gradient, part, tile_num):
    tokens = queries.shape[0]
    width = GROUP * HEAD_WIDTH
    block = pl.BlockSpec((tokens, width), lambda i: (0, 2 * i + part))
    fixed = lambda shape: pl.BlockSpec(shape, lambda i: (0, 0))
    out_specs = [pl.BlockSpec((tile_num, CAP * GROUP, 2 * HEAD_WIDTH), lambda i: (i, 0, 0))]
    out_shape = [jax.ShapeDtypeStruct((2 * tile_num, CAP * GROUP, 2 * HEAD_WIDTH), BF16)]
    if part == 0:
        for shape in ((tile_num * CAP, tokens), (tokens, tile_num * CAP)):
            out_specs.append(fixed(shape))
            out_shape.append(jax.ShapeDtypeStruct(shape, BF16))
    return pl.pallas_call(
        route_kernel if part == 0 else dispatch_kernel,
        grid=(2,),
        in_specs=[fixed(routing.shape), block, block],
        out_specs=out_specs,
        out_shape=out_shape,
        scratch_shapes=[pltpu.VMEM((tile_num * GROUP, HEAD_WIDTH), F32)],
        compiler_params=pltpu.CompilerParams(vmem_limit_bytes=LIMIT),
        cost_estimate=pl.CostEstimate(flops=10**9, bytes_accessed=3 * 10**6, transcendentals=0),
        name="dispatch",
    )(routing, queries, output_gradient)


def combine_kernel(turned_ref, back_ref, *refs):
    attended_ref, query_grad_ref, ninth_ref = refs[-3:]
    tile_num = back_ref.shape[0]
    for t in range(tile_num):
        last = back_ref[t, MAIN * GROUP :, :].astype(F32)
        ninth_ref[0, t * GROUP : (t + 1) * GROUP, :] = last[:, :HEAD_WIDTH]
        ninth_ref[1, t * GROUP : (t + 1) * GROUP, :] = last[:, HEAD_WIDTH:]
    for h in range(GROUP):
        lanes = slice(h * HEAD_WIDTH, (h + 1) * HEAD_WIDTH)
        parts = [back_ref[t, h * MAIN : (h + 1) * MAIN, :].astype(F32) for t in range(tile_num)]
        main = jnp.concatenate(parts, axis=0)
        for side, target in ((0, attended_ref), (1, query_grad_ref)):
            ninth = ninth_ref[side, pl.ds(h, tile_num, stride=GROUP), :]
            half = main[:, side * HEAD_WIDTH : (side + 1) * HEAD_WIDTH]
            rows = jnp.concatenate([half, ninth], axis=0).astype(BF16)
            target[:, lanes] = jnp.dot(
                turned_ref[...], rows, preferred_element_type=F32
            ).astype(BF16)


def combine(turned, back, part, earlier, shape):
    tokens = shape[0]
    tile_num = back.shape[0] // 2
    width = GROUP * HEAD_WIDTH
    block = pl.BlockSpec((tokens, width), lambda i: (0, 2 * i + part))
    whole = pl.BlockSpec(memory_space=pl.ANY)
    return pl.pallas_call(
        combine_kernel,
        grid=(2,),
        in_specs=[
            pl.BlockSpec(turned.shape, lambda i: (0, 0)),
            pl.BlockSpec((tile_num, CAP * GROUP, 2 * HEAD_WIDTH), lambda i: (i, 0, 0)),
        ]
        + [whole] * len(earlier),
        out_specs=[block, block],
        out_shape=[jax.ShapeDtypeStruct(shape, BF16)] * 2,
        scratch_shapes=[pltpu.VMEM((2, tile_num * GROUP, HEAD_WIDTH), F32)],
        input_output_aliases={2: 0, 3: 1} if earlier else {},
        compiler_params=pltpu.CompilerParams(vmem_limit_bytes=SMALL),
        cost_estimate=pl.CostEstimate(flops=10**6, bytes_accessed=10**5, transcendentals=0),
        name="combine",
    )(turned, back, *earlier)


def attend_kernel(info, rows_ref, key_ref, value_ref, back_ref, *refs, ways, depth):
    scratch = refs[-(10 + sum(TURNS)) :]
    shares = refs[: -len(scratch)]
    query_s, grad_s, out_s, query_grad_s, key_fill, key_zero, value_ones = scratch[:7]
    key_grad_s, value_grad_s, grads_s = scratch[7:10]
    buffers = list(scratch[10:])
    turns = [[buffers.pop(0) for _ in range(turn)] for turn in TURNS]
    score_s, prob_s, slope_s = ([turn[w % len(turn)] for w in range(ways)] for turn in turns)
    device_num, slot_rows, _ = rows_ref.shape
    patches = key_ref.shape[1]
    width = HEAD_WIDTH
    block_rows = query_s.shape[0] // ways
    inv_root = 1.0 / math.sqrt(width)
    to_power = math.log2(math.e) * inv_root

    live = lax.broadcasted_iota(jnp.int32, (patches, width), 0) < info[2]
    key, value = key_ref[0].astype(F32), value_ref[0].astype(F32)
    key_fill[...] = jnp.where(live, key, key[0:1, :]).astype(BF16)
    key_zero[...] = jnp.where(live, key, 0.0).astype(BF16)
    value_ones[:, :width] = jnp.where(live, value, 0.0).astype(BF16)
    value_ones[:, width:] = jnp.where(live, 1.0, 0.0).astype(BF16)
    for i in range(0, device_num, 2):
        for first, target in ((0, query_s), (width, grad_s)):
            pair = [rows_ref[i + j, :, first : first + width].astype(F32) for j in range(2)]
            target[i * slot_rows : (i + 2) * slot_rows, :] = jnp.concatenate(pair, axis=0).astype(BF16)
    key_grad_s[...] = jnp.zeros_like(key_grad_s)
    value_grad_s[...] = jnp.zeros_like(value_grad_s)

    here = [slice(w * block_rows, (w + 1) * block_rows) for w in range(ways)]
    peak, grad, grad_dot = {}, {}, {}

    def scores(w):
        score = lax.dot_general(
            query_s[here[w], :], key_fill[...], ROWS_LAST, preferred_element_type=F32
        )
        score_s[w][...] = score
        peak[w] = jnp.max(score, axis=1, keepdims=True) * to_power

    def weights(w):
        prob_s[w][...] = jnp.exp2(score_s[w][...] * to_power - peak[w]).astype(BF16)

    def output(w):
        mixed = jnp.dot(prob_s[w][...], value_ones[...], preferred_element_type=F32)
        scale = 1.0 / mixed[:, width:]
        attended = (mixed[:, :width] * scale).astype(BF16).astype(F32)
        out_s[here[w], :] = attended
        grad[w] = (grad_s[here[w], :].astype(F32) * scale).astype(BF16)
        grad_dot[w] = jnp.sum(grad[w].astype(F32) * attended, axis=1, keepdims=True)

    def slopes(w):
        prob_grad = lax.dot_general(
            grad[w], value_ones[:, :width], ROWS_LAST, preferred_element_type=F32
        )
        slope_s[w][...] = (prob_grad - grad_dot[w]).astype(BF16) * prob_s[w][...]

    def value_term(w):
        turned = grad[w].astype(F32).T.astype(BF16)
        value_grad_s[...] += jnp.dot(turned, prob_s[w][...], preferred_element_type=F32)

    def query_term(w):
        query_grad_s[here[w], :] = inv_root * jnp.dot(
            slope_s[w][...], key_zero[...], preferred_element_type=F32
        )

    def key_term(w):
        turned = query_s[here[w], :].astype(F32).T.astype(BF16)
        key_grad_s[...] += jnp.dot(turned, slope_s[w][...], preferred_element_type=F32)

    steps = (scores, weights, output, slopes, value_term, query_term, key_term)
    for now in range(len(steps) + ways - 1):
        for w in range(ways):
            if 0 <= now - w < len(steps):
                steps[now - w](w)

    for i in range(device_num):
        own = slice(i * slot_rows, (i + 1) * slot_rows)
        back_ref[i, :, :width] = out_s[own, :].astype(BF16)
        back_ref[i, :, width:] = query_grad_s[own, :].astype(BF16)
    live = lax.broadcasted_iota(jnp.int32, (width, patches), 1) < info[2]
    grads_s[:, :width] = jnp.where(live, key_grad_s[...] * inv_root, 0.0).T
    grads_s[:, width:] = jnp.where(live, value_grad_s[...], 0.0).T
    for i, share in enumerate(shares):
        size = share.shape[0]
        split = len(shares) // depth
        place = lax.rem(info[1] + i // split, depth) * split
        if split == 2:
            place = place + (info[0] if i % 2 == 0 else 1 - info[0])
        share[...] = grads_s[pl.ds(pl.multiple_of(place * size, size), size), :].astype(BF16)


def attend(info, rows, keys, values, depth, split):
    device_num, slot_rows, both = rows.shape
    patches = keys.shape[1]
    share_num = depth * split
    total = device_num * slot_rows
    width = HEAD_WIDTH
    share = patches // share_num
    ways = WAYS
    block_rows = total // ways
    tile = pl.BlockSpec((1, patches, width), lambda i, info: (0, 0, 0))
    whole = pl.BlockSpec(rows.shape, lambda i, info: (0, 0, 0))
    return pl.pallas_call(
        functools.partial(attend_kernel, ways=ways, depth=depth),
        grid_spec=pltpu.PrefetchScalarGridSpec(
            num_scalar_prefetch=1,
            grid=(1,),
            in_specs=[whole, tile, tile],
            out_specs=[whole] + [pl.BlockSpec((share, both), lambda i, info: (0, 0))] * share_num,
            scratch_shapes=[
                pltpu.VMEM((total, width), BF16),
                pltpu.VMEM((total, width), BF16),
                pltpu.VMEM((total, width), F32),
                pltpu.VMEM((total, width), F32),
                pltpu.VMEM((patches, width), BF16),
                pltpu.VMEM((patches, width), BF16),
                pltpu.VMEM((patches, both), BF16),
                pltpu.VMEM((width, patches), F32),
                pltpu.VMEM((width, patches), F32),
                pltpu.VMEM((patches, both), F32),
            ]
            + [pltpu.VMEM((block_rows, patches), F32)] * TURNS[0]
            + [pltpu.VMEM((block_rows, patches), BF16)] * (TURNS[1] + TURNS[2]),
        ),
        out_shape=[jax.ShapeDtypeStruct(rows.shape, BF16)]
        + [jax.ShapeDtypeStruct((share, both), BF16)] * share_num,
        compiler_params=pltpu.CompilerParams(vmem_limit_bytes=ATTEND_LIMITS[split - 1]),
        cost_estimate=pl.CostEstimate(
            flops=60 * total * patches * width,
            bytes_accessed=4 * 10**6,
            transcendentals=total * patches,
        ),
        name="attend",
    )(info, rows, keys, values)


def add_kernel(info, *refs):
    shares, (mine_ref, theirs_ref) = refs[:-2], refs[-2:]
    half = mine_ref.shape[0]
    for target, core in ((mine_ref, info[0]), (theirs_ref, 1 - info[0])):
        rows = pl.ds(pl.multiple_of(core * half, half), half)
        target[...] = sum(share[rows, :].astype(F32) for share in shares).astype(target.dtype)


def add_shares(info, shares):
    rows, both = shares[0].shape
    half = rows // 2
    fixed = lambda size: pl.BlockSpec((size, both), lambda i, info: (0, 0))
    return pl.pallas_call(
        add_kernel,
        grid_spec=pltpu.PrefetchScalarGridSpec(
            num_scalar_prefetch=1,
            grid=(1,),
            in_specs=[fixed(rows)] * len(shares),
            out_specs=[fixed(half)] * 2,
        ),
        out_shape=[jax.ShapeDtypeStruct((half, both), dtype) for dtype in (F32, BF16)],
        compiler_params=pltpu.CompilerParams(vmem_limit_bytes=SMALL),
        cost_estimate=pl.CostEstimate(flops=10**6, bytes_accessed=10**5, transcendentals=0),
        name="add_shares",
    )(info, *shares)


def place_kernel(info, *refs):
    (mine, other, *shares), (key_ref, value_ref) = refs[:-2], refs[-2:]
    width = HEAD_WIDTH
    parts = [(mine[...], other[...].astype(F32))]
    parts.append([sum(share[...].astype(F32) for share in shares[i::2]) for i in range(2)])
    for part, (own, theirs) in enumerate(parts):
        for core in range(2):
            chosen = jnp.where(info[0] == core, own, theirs)
            group = 2 * core + part
            for first, target in ((0, key_ref), (width, value_ref)):
                target[0, :, group * width : (group + 1) * width] = chosen[:, first : first + width]


def place(info, mine, other, shares):
    rows, both = mine.shape
    out = (1, rows, 2 * both)
    return pl.pallas_call(
        place_kernel,
        grid_spec=pltpu.PrefetchScalarGridSpec(
            num_scalar_prefetch=1,
            grid=(1,),
            in_specs=[pl.BlockSpec((rows, both), lambda i, info: (0, 0))] * (2 + len(shares)),
            out_specs=[pl.BlockSpec(out, lambda i, info: (0, 0, 0))] * 2,
        ),
        out_shape=[jax.ShapeDtypeStruct(out, F32)] * 2,
        compiler_params=pltpu.CompilerParams(vmem_limit_bytes=SMALL),
        cost_estimate=pl.CostEstimate(flops=10**6, bytes_accessed=10**5, transcendentals=0),
        name="place",
    )(info, mine, other, *shares)


def local(queries, tile_ids, keys, values, patch_counts, output_gradient):
    tile_num = lax.axis_size("img")
    depth = lax.axis_size("z")
    info = jnp.stack([lax.axis_index("core"), lax.axis_index("z"), patch_counts[0]]).astype(jnp.int32)
    exchange = functools.partial(
        lax.all_to_all, axis_name=("core", "img"), split_axis=0, concat_axis=0, tiled=True
    )
    ids = tile_ids.reshape(1, -1)
    sent, slots, turned = dispatch(ids, queries, output_gradient, 0, tile_num)
    (later,) = dispatch(slots, queries, output_gradient, 1, tile_num)
    first = 2 * lax.axis_index("core") * HEAD_WIDTH
    tiles = [
        [lax.dynamic_slice_in_dim(a, first + part * HEAD_WIDTH, HEAD_WIDTH, 2) for a in (keys, values)]
        for part in range(2)
    ]
    rows, later, tiles = lax.optimization_barrier((exchange(sent), later, tiles))
    rows = [rows, exchange(later)]
    back, *shares = attend(info, rows[0], *tiles[0], depth, 1)
    first_back = exchange(back)
    along_z = lambda share, i: lax.ppermute(share, "z", [(z, (z + i) % depth) for z in range(depth)])
    early, late = ((1, 3), (2,))
    for i in early:
        shares[i] = along_z(shares[i], i)
    waiting, rows = lax.optimization_barrier(([shares[i] for i in late], rows))
    for i, share in zip(late, waiting):
        shares[i] = along_z(share, i)
    back, *later = attend(info, rows[1], *tiles[1], depth, 2)
    back, shares = lax.optimization_barrier((back, shares))
    second_back = exchange(back)
    for i in range(1, 2 * depth):
        to = lambda z, core: ((z + i // 2) % depth) * 2 + (core + i) % 2
        pairs = [(2 * z + core, to(z, core)) for z in range(depth) for core in range(2)]
        later[i] = lax.ppermute(later[i], ("z", "core"), pairs)
    mine, given = add_shares(info, shares)
    other = lax.ppermute(given, "core", [(0, 1), (1, 0)])
    outputs = combine(turned, first_back, 0, (), queries.shape)
    grads = place(info, mine, other, later)
    outputs = combine(turned, second_back, 1, outputs, queries.shape)
    return (*outputs, *grads)


def solution(mesh):
    ctx, img = mesh.devices.shape
    fine = Mesh(mesh.devices.reshape(ctx // 2, 2, img), ("z", "core", "img"))
    rows = P(("z", "core", "img"), None)
    grads = P("img", ("z", "core"), None)
    tiles = P("img", None, None)
    return jax.shard_map(
        local,
        mesh=fine,
        in_specs=(rows, rows, tiles, tiles, P("img"), rows),
        out_specs=(rows, rows, grads, grads),
        check_vma=False,
    )
```

```python
import functools
import math

import jax
import jax.numpy as jnp
from jax import lax
from jax.experimental import pallas as pl
from jax.experimental.pallas import tpu as pltpu
from jax.sharding import Mesh, PartitionSpec as P

HEAD_WIDTH = 128
GROUP = 8
CAP = 9
MAIN = 8
F32 = jnp.float32
BF16 = jnp.bfloat16
ROWS_LAST = (((1,), (1,)), ((), ()))
LIMIT = 60 * 2**20
SMALL = 16 * 2**20
ATTEND_LIMITS = (32 * 2**20, 32 * 2**20)
WAYS = 9
TURNS = (3, 5, 5)


def token_slots(ids, tile_num):
    tokens = ids.shape[1]
    chosen = jnp.where(ids == lax.broadcasted_iota(jnp.int32, (128, tokens), 0), 1.0, 0.0)
    row = lax.broadcasted_iota(jnp.int32, (tokens, tokens), 0)
    column = lax.broadcasted_iota(jnp.int32, (tokens, tokens), 1)
    earlier = jnp.where(row < column, 1.0, 0.0).astype(BF16)
    before = jnp.dot(chosen.astype(BF16), earlier, preferred_element_type=F32)
    place = jnp.where(chosen > 0.0, before, -1.0).astype(BF16)
    slots = tile_num * CAP
    slot = lax.broadcasted_iota(jnp.int32, (slots, 128), 0)
    ninth = slot >= tile_num * MAIN
    tile = jnp.where(ninth, slot - tile_num * MAIN, slot // MAIN)
    spread = jnp.where(tile == lax.broadcasted_iota(jnp.int32, (slots, 128), 1), 1.0, 0.0)
    held = jnp.dot(spread.astype(BF16), place, preferred_element_type=F32)
    turn = jnp.where(ninth, MAIN, slot % MAIN).astype(F32)
    return jnp.where(held == turn, 1.0, 0.0)


def route_kernel(ids_ref, query_ref, grad_ref, sent_ref, slots_ref, turned_ref, ninth_ref):
    @pl.when(pl.program_id(0) == 0)
    def _():
        slots = token_slots(ids_ref[...], sent_ref.shape[0])
        slots_ref[...] = slots.astype(BF16)
        turned_ref[...] = slots.T.astype(BF16)

    dispatch_kernel(slots_ref, query_ref, grad_ref, sent_ref, ninth_ref)


def dispatch_kernel(slots_ref, query_ref, grad_ref, sent_ref, ninth_ref):
    tile_num = sent_ref.shape[0]
    for first, source in ((0, query_ref), (HEAD_WIDTH, grad_ref)):
        lanes = slice(first, first + HEAD_WIDTH)
        rows = jnp.dot(slots_ref[...], source[...], preferred_element_type=F32)
        heads = [rows[:, h * HEAD_WIDTH : (h + 1) * HEAD_WIDTH] for h in range(GROUP)]
        for h in range(GROUP):
            ninth_ref[pl.ds(h, tile_num, stride=GROUP), :] = heads[h][tile_num * MAIN :]
        for t in range(tile_num):
            parts = [head[t * MAIN : (t + 1) * MAIN] for head in heads]
            parts.append(ninth_ref[t * GROUP : (t + 1) * GROUP, :])
            sent_ref[t, :, lanes] = jnp.concatenate(parts, axis=0).astype(BF16)


def dispatch(routing, queries, output_gradient, part, tile_num):
    tokens = queries.shape[0]
    width = GROUP * HEAD_WIDTH
    block = pl.BlockSpec((tokens, width), lambda i: (0, 2 * i + part))
    fixed = lambda shape: pl.BlockSpec(shape, lambda i: (0, 0))
    out_specs = [pl.BlockSpec((tile_num, CAP * GROUP, 2 * HEAD_WIDTH), lambda i: (i, 0, 0))]
    out_shape = [jax.ShapeDtypeStruct((2 * tile_num, CAP * GROUP, 2 * HEAD_WIDTH), BF16)]
    if part == 0:
        for shape in ((tile_num * CAP, tokens), (tokens, tile_num * CAP)):
            out_specs.append(fixed(shape))
            out_shape.append(jax.ShapeDtypeStruct(shape, BF16))
    return pl.pallas_call(
        route_kernel if part == 0 else dispatch_kernel,
        grid=(2,),
        in_specs=[fixed(routing.shape), block, block],
        out_specs=out_specs,
        out_shape=out_shape,
        scratch_shapes=[pltpu.VMEM((tile_num * GROUP, HEAD_WIDTH), F32)],
        compiler_params=pltpu.CompilerParams(vmem_limit_bytes=LIMIT),
        cost_estimate=pl.CostEstimate(flops=10**9, bytes_accessed=3 * 10**6, transcendentals=0),
        name="dispatch",
    )(routing, queries, output_gradient)


def combine_kernel(turned_ref, back_ref, *refs):
    attended_ref, query_grad_ref, ninth_ref = refs[-3:]
    tile_num = back_ref.shape[0]
    for t in range(tile_num):
        last = back_ref[t, MAIN * GROUP :, :].astype(F32)
        ninth_ref[0, t * GROUP : (t + 1) * GROUP, :] = last[:, :HEAD_WIDTH]
        ninth_ref[1, t * GROUP : (t + 1) * GROUP, :] = last[:, HEAD_WIDTH:]
    for h in range(GROUP):
        lanes = slice(h * HEAD_WIDTH, (h + 1) * HEAD_WIDTH)
        parts = [back_ref[t, h * MAIN : (h + 1) * MAIN, :].astype(F32) for t in range(tile_num)]
        main = jnp.concatenate(parts, axis=0)
        for side, target in ((0, attended_ref), (1, query_grad_ref)):
            ninth = ninth_ref[side, pl.ds(h, tile_num, stride=GROUP), :]
            half = main[:, side * HEAD_WIDTH : (side + 1) * HEAD_WIDTH]
            rows = jnp.concatenate([half, ninth], axis=0).astype(BF16)
            target[:, lanes] = jnp.dot(
                turned_ref[...], rows, preferred_element_type=F32
            ).astype(BF16)


def combine(turned, back, part, earlier, shape):
    tokens = shape[0]
    tile_num = back.shape[0] // 2
    width = GROUP * HEAD_WIDTH
    block = pl.BlockSpec((tokens, width), lambda i: (0, 2 * i + part))
    whole = pl.BlockSpec(memory_space=pl.ANY)
    return pl.pallas_call(
        combine_kernel,
        grid=(2,),
        in_specs=[
            pl.BlockSpec(turned.shape, lambda i: (0, 0)),
            pl.BlockSpec((tile_num, CAP * GROUP, 2 * HEAD_WIDTH), lambda i: (i, 0, 0)),
        ]
        + [whole] * len(earlier),
        out_specs=[block, block],
        out_shape=[jax.ShapeDtypeStruct(shape, BF16)] * 2,
        scratch_shapes=[pltpu.VMEM((2, tile_num * GROUP, HEAD_WIDTH), F32)],
        input_output_aliases={2: 0, 3: 1} if earlier else {},
        compiler_params=pltpu.CompilerParams(vmem_limit_bytes=SMALL),
        cost_estimate=pl.CostEstimate(flops=10**6, bytes_accessed=10**5, transcendentals=0),
        name="combine",
    )(turned, back, *earlier)


def attend_kernel(info, rows_ref, key_ref, value_ref, back_ref, *refs, ways, depth):
    scratch = refs[-(10 + sum(TURNS)) :]
    shares = refs[: -len(scratch)]
    query_s, grad_s, out_s, query_grad_s, key_fill, key_zero, value_ones = scratch[:7]
    key_grad_s, value_grad_s, grads_s = scratch[7:10]
    buffers = list(scratch[10:])
    turns = [[buffers.pop(0) for _ in range(turn)] for turn in TURNS]
    score_s, prob_s, slope_s = ([turn[w % len(turn)] for w in range(ways)] for turn in turns)
    device_num, slot_rows, _ = rows_ref.shape
    patches = key_ref.shape[1]
    width = HEAD_WIDTH
    block_rows = query_s.shape[0] // ways
    inv_root = 1.0 / math.sqrt(width)
    to_power = math.log2(math.e) * inv_root

    live = lax.broadcasted_iota(jnp.int32, (patches, width), 0) < info[2]
    key, value = key_ref[0].astype(F32), value_ref[0].astype(F32)
    key_fill[...] = jnp.where(live, key, key[0:1, :]).astype(BF16)
    key_zero[...] = jnp.where(live, key, 0.0).astype(BF16)
    value_ones[:, :width] = jnp.where(live, value, 0.0).astype(BF16)
    value_ones[:, width:] = jnp.where(live, 1.0, 0.0).astype(BF16)
    for i in range(0, device_num, 2):
        for first, target in ((0, query_s), (width, grad_s)):
            pair = [rows_ref[i + j, :, first : first + width].astype(F32) for j in range(2)]
            target[i * slot_rows : (i + 2) * slot_rows, :] = jnp.concatenate(pair, axis=0).astype(BF16)
    key_grad_s[...] = jnp.zeros_like(key_grad_s)
    value_grad_s[...] = jnp.zeros_like(value_grad_s)

    here = [slice(w * block_rows, (w + 1) * block_rows) for w in range(ways)]
    peak, grad, grad_dot = {}, {}, {}

    def scores(w):
        score = lax.dot_general(
            query_s[here[w], :], key_fill[...], ROWS_LAST, preferred_element_type=F32
        )
        score_s[w][...] = score
        peak[w] = jnp.max(score, axis=1, keepdims=True) * to_power

    def weights(w):
        prob_s[w][...] = jnp.exp2(score_s[w][...] * to_power - peak[w]).astype(BF16)

    def output(w):
        mixed = jnp.dot(prob_s[w][...], value_ones[...], preferred_element_type=F32)
        scale = 1.0 / mixed[:, width:]
        attended = (mixed[:, :width] * scale).astype(BF16).astype(F32)
        out_s[here[w], :] = attended
        grad[w] = (grad_s[here[w], :].astype(F32) * scale).astype(BF16)
        grad_dot[w] = jnp.sum(grad[w].astype(F32) * attended, axis=1, keepdims=True)

    def slopes(w):
        prob_grad = lax.dot_general(
            grad[w], value_ones[:, :width], ROWS_LAST, preferred_element_type=F32
        )
        slope_s[w][...] = (prob_grad - grad_dot[w]).astype(BF16) * prob_s[w][...]

    def value_term(w):
        turned = grad[w].astype(F32).T.astype(BF16)
        value_grad_s[...] += jnp.dot(turned, prob_s[w][...], preferred_element_type=F32)

    def query_term(w):
        query_grad_s[here[w], :] = inv_root * jnp.dot(
            slope_s[w][...], key_zero[...], preferred_element_type=F32
        )

    def key_term(w):
        turned = query_s[here[w], :].astype(F32).T.astype(BF16)
        key_grad_s[...] += jnp.dot(turned, slope_s[w][...], preferred_element_type=F32)

    steps = (scores, weights, output, slopes, value_term, query_term, key_term)
    for now in range(len(steps) + ways - 1):
        for w in range(ways):
            if 0 <= now - w < len(steps):
                steps[now - w](w)

    for i in range(device_num):
        own = slice(i * slot_rows, (i + 1) * slot_rows)
        back_ref[i, :, :width] = out_s[own, :].astype(BF16)
        back_ref[i, :, width:] = query_grad_s[own, :].astype(BF16)
    live = lax.broadcasted_iota(jnp.int32, (width, patches), 1) < info[2]
    grads_s[:, :width] = jnp.where(live, key_grad_s[...] * inv_root, 0.0).T
    grads_s[:, width:] = jnp.where(live, value_grad_s[...], 0.0).T
    for i, share in enumerate(shares):
        size = share.shape[0]
        split = len(shares) // depth
        place = lax.rem(info[1] + i // split, depth) * split
        if split == 2:
            place = place + (info[0] if i % 2 == 0 else 1 - info[0])
        share[...] = grads_s[pl.ds(pl.multiple_of(place * size, size), size), :].astype(BF16)


def attend(info, rows, keys, values, depth, split):
    device_num, slot_rows, both = rows.shape
    patches = keys.shape[1]
    share_num = depth * split
    total = device_num * slot_rows
    width = HEAD_WIDTH
    share = patches // share_num
    ways = WAYS
    block_rows = total // ways
    tile = pl.BlockSpec((1, patches, width), lambda i, info: (0, 0, 0))
    whole = pl.BlockSpec(rows.shape, lambda i, info: (0, 0, 0))
    return pl.pallas_call(
        functools.partial(attend_kernel, ways=ways, depth=depth),
        grid_spec=pltpu.PrefetchScalarGridSpec(
            num_scalar_prefetch=1,
            grid=(1,),
            in_specs=[whole, tile, tile],
            out_specs=[whole] + [pl.BlockSpec((share, both), lambda i, info: (0, 0))] * share_num,
            scratch_shapes=[
                pltpu.VMEM((total, width), BF16),
                pltpu.VMEM((total, width), BF16),
                pltpu.VMEM((total, width), F32),
                pltpu.VMEM((total, width), F32),
                pltpu.VMEM((patches, width), BF16),
                pltpu.VMEM((patches, width), BF16),
                pltpu.VMEM((patches, both), BF16),
                pltpu.VMEM((width, patches), F32),
                pltpu.VMEM((width, patches), F32),
                pltpu.VMEM((patches, both), F32),
            ]
            + [pltpu.VMEM((block_rows, patches), F32)] * TURNS[0]
            + [pltpu.VMEM((block_rows, patches), BF16)] * (TURNS[1] + TURNS[2]),
        ),
        out_shape=[pltpu.HBM(rows.shape, BF16)] + [pltpu.HBM((share, both), BF16)] * share_num,
        compiler_params=pltpu.CompilerParams(vmem_limit_bytes=ATTEND_LIMITS[split - 1]),
        cost_estimate=pl.CostEstimate(
            flops=60 * total * patches * width,
            bytes_accessed=4 * 10**6,
            transcendentals=total * patches,
        ),
        name="attend",
    )(info, rows, keys, values)


def add_kernel(info, *refs):
    shares, (mine_ref, theirs_ref) = refs[:-2], refs[-2:]
    half = mine_ref.shape[0]
    for target, core in ((mine_ref, info[0]), (theirs_ref, 1 - info[0])):
        rows = pl.ds(pl.multiple_of(core * half, half), half)
        target[...] = sum(share[rows, :].astype(F32) for share in shares).astype(target.dtype)


def add_shares(info, shares):
    rows, both = shares[0].shape
    half = rows // 2
    fixed = lambda size: pl.BlockSpec((size, both), lambda i, info: (0, 0))
    return pl.pallas_call(
        add_kernel,
        grid_spec=pltpu.PrefetchScalarGridSpec(
            num_scalar_prefetch=1,
            grid=(1,),
            in_specs=[fixed(rows)] * len(shares),
            out_specs=[fixed(half)] * 2,
        ),
        out_shape=[jax.ShapeDtypeStruct((half, both), dtype) for dtype in (F32, BF16)],
        compiler_params=pltpu.CompilerParams(vmem_limit_bytes=SMALL),
        cost_estimate=pl.CostEstimate(flops=10**6, bytes_accessed=10**5, transcendentals=0),
        name="add_shares",
    )(info, *shares)


def place_kernel(info, *refs):
    (mine, other, *shares), (key_ref, value_ref) = refs[:-2], refs[-2:]
    width = HEAD_WIDTH
    parts = [(mine[...], other[...].astype(F32))]
    parts.append([sum(share[...].astype(F32) for share in shares[i::2]) for i in range(2)])
    for part, (own, theirs) in enumerate(parts):
        for core in range(2):
            chosen = jnp.where(info[0] == core, own, theirs)
            group = 2 * core + part
            for first, target in ((0, key_ref), (width, value_ref)):
                target[0, :, group * width : (group + 1) * width] = chosen[:, first : first + width]


def place(info, mine, other, shares):
    rows, both = mine.shape
    out = (1, rows, 2 * both)
    return pl.pallas_call(
        place_kernel,
        grid_spec=pltpu.PrefetchScalarGridSpec(
            num_scalar_prefetch=1,
            grid=(1,),
            in_specs=[pl.BlockSpec((rows, both), lambda i, info: (0, 0))] * (2 + len(shares)),
            out_specs=[pl.BlockSpec(out, lambda i, info: (0, 0, 0))] * 2,
        ),
        out_shape=[jax.ShapeDtypeStruct(out, F32)] * 2,
        compiler_params=pltpu.CompilerParams(vmem_limit_bytes=SMALL),
        cost_estimate=pl.CostEstimate(flops=10**6, bytes_accessed=10**5, transcendentals=0),
        name="place",
    )(info, mine, other, *shares)


def local(queries, tile_ids, keys, values, patch_counts, output_gradient):
    tile_num = lax.axis_size("img")
    depth = lax.axis_size("z")
    info = jnp.stack([lax.axis_index("core"), lax.axis_index("z"), patch_counts[0]]).astype(jnp.int32)
    exchange = functools.partial(
        lax.all_to_all, axis_name=("core", "img"), split_axis=0, concat_axis=0, tiled=True
    )
    ids = tile_ids.reshape(1, -1)
    sent, slots, turned = dispatch(ids, queries, output_gradient, 0, tile_num)
    (later,) = dispatch(slots, queries, output_gradient, 1, tile_num)
    first = 2 * lax.axis_index("core") * HEAD_WIDTH
    tiles = [
        [lax.dynamic_slice_in_dim(a, first + part * HEAD_WIDTH, HEAD_WIDTH, 2) for a in (keys, values)]
        for part in range(2)
    ]
    rows, later, tiles = lax.optimization_barrier((exchange(sent), later, tiles))
    rows = [rows, exchange(later)]
    back, *shares = attend(info, rows[0], *tiles[0], depth, 1)
    first_back = exchange(back)
    along_z = lambda share, i: lax.ppermute(share, "z", [(z, (z + i) % depth) for z in range(depth)])
    early, late = ((1, 3), (2,))
    for i in early:
        shares[i] = along_z(shares[i], i)
    waiting, rows = lax.optimization_barrier(([shares[i] for i in late], rows))
    for i, share in zip(late, waiting):
        shares[i] = along_z(share, i)
    back, *later = attend(info, rows[1], *tiles[1], depth, 2)
    back, shares = lax.optimization_barrier((back, shares))
    second_back = exchange(back)
    for i in range(1, 2 * depth):
        to = lambda z, core: ((z + i // 2) % depth) * 2 + (core + i) % 2
        pairs = [(2 * z + core, to(z, core)) for z in range(depth) for core in range(2)]
        later[i] = lax.ppermute(later[i], ("z", "core"), pairs)
    mine, given = add_shares(info, shares)
    other = lax.ppermute(given, "core", [(0, 1), (1, 0)])
    outputs = combine(turned, first_back, 0, (), queries.shape)
    grads = place(info, mine, other, later)
    outputs = combine(turned, second_back, 1, outputs, queries.shape)
    return (*outputs, *grads)


def solution(mesh):
    ctx, img = mesh.devices.shape
    fine = Mesh(mesh.devices.reshape(ctx // 2, 2, img), ("z", "core", "img"))
    rows = P(("z", "core", "img"), None)
    grads = P("img", ("z", "core"), None)
    tiles = P("img", None, None)
    return jax.shard_map(
        local,
        mesh=fine,
        in_specs=(rows, rows, tiles, tiles, P("img"), rows),
        out_specs=(rows, rows, grads, grads),
        check_vma=False,
    )
```

```python
import functools
import math

import jax
import jax.numpy as jnp
from jax import lax
from jax.experimental import pallas as pl
from jax.experimental.pallas import tpu as pltpu
from jax.sharding import Mesh, PartitionSpec as P

HEAD_WIDTH = 128
GROUP = 8
CAP = 9
MAIN = 8
F32 = jnp.float32
BF16 = jnp.bfloat16
ROWS_LAST = (((1,), (1,)), ((), ()))
LIMIT = 60 * 2**20
SMALL = 16 * 2**20
ATTEND_LIMITS = (32 * 2**20, 32 * 2**20)
WAYS = 9
TURNS = (3, 5, 5)


def token_slots(ids, tile_num):
    tokens = ids.shape[1]
    chosen = jnp.where(ids == lax.broadcasted_iota(jnp.int32, (128, tokens), 0), 1.0, 0.0)
    row = lax.broadcasted_iota(jnp.int32, (tokens, tokens), 0)
    column = lax.broadcasted_iota(jnp.int32, (tokens, tokens), 1)
    earlier = jnp.where(row < column, 1.0, 0.0).astype(BF16)
    before = jnp.dot(chosen.astype(BF16), earlier, preferred_element_type=F32)
    place = jnp.where(chosen > 0.0, before, -1.0).astype(BF16)
    slots = tile_num * CAP
    slot = lax.broadcasted_iota(jnp.int32, (slots, 128), 0)
    ninth = slot >= tile_num * MAIN
    tile = jnp.where(ninth, slot - tile_num * MAIN, slot // MAIN)
    spread = jnp.where(tile == lax.broadcasted_iota(jnp.int32, (slots, 128), 1), 1.0, 0.0)
    held = jnp.dot(spread.astype(BF16), place, preferred_element_type=F32)
    turn = jnp.where(ninth, MAIN, slot % MAIN).astype(F32)
    return jnp.where(held == turn, 1.0, 0.0)


def route_kernel(ids_ref, query_ref, grad_ref, sent_ref, slots_ref, ninth_ref):
    @pl.when(pl.program_id(0) == 0)
    def _():
        slots_ref[...] = token_slots(ids_ref[...], sent_ref.shape[0]).astype(BF16)

    dispatch_kernel(slots_ref, query_ref, grad_ref, sent_ref, ninth_ref)


def turn_kernel(slots_ref, query_ref, grad_ref, sent_ref, turned_ref, ninth_ref):
    @pl.when(pl.program_id(0) == 0)
    def _():
        turned_ref[...] = slots_ref[...].astype(F32).T.astype(BF16)

    dispatch_kernel(slots_ref, query_ref, grad_ref, sent_ref, ninth_ref)


def dispatch_kernel(slots_ref, query_ref, grad_ref, sent_ref, ninth_ref):
    tile_num = sent_ref.shape[0]
    for first, source in ((0, query_ref), (HEAD_WIDTH, grad_ref)):
        lanes = slice(first, first + HEAD_WIDTH)
        rows = jnp.dot(slots_ref[...], source[...], preferred_element_type=F32)
        heads = [rows[:, h * HEAD_WIDTH : (h + 1) * HEAD_WIDTH] for h in range(GROUP)]
        for h in range(GROUP):
            ninth_ref[pl.ds(h, tile_num, stride=GROUP), :] = heads[h][tile_num * MAIN :]
        for t in range(tile_num):
            parts = [head[t * MAIN : (t + 1) * MAIN] for head in heads]
            parts.append(ninth_ref[t * GROUP : (t + 1) * GROUP, :])
            sent_ref[t, :, lanes] = jnp.concatenate(parts, axis=0).astype(BF16)


def dispatch(routing, queries, output_gradient, part, tile_num):
    tokens = queries.shape[0]
    width = GROUP * HEAD_WIDTH
    block = pl.BlockSpec((tokens, width), lambda i: (0, 2 * i + part))
    fixed = lambda shape: pl.BlockSpec(shape, lambda i: (0, 0))
    out_specs = [pl.BlockSpec((tile_num, CAP * GROUP, 2 * HEAD_WIDTH), lambda i: (i, 0, 0))]
    out_shape = [jax.ShapeDtypeStruct((2 * tile_num, CAP * GROUP, 2 * HEAD_WIDTH), BF16)]
    shape = (tile_num * CAP, tokens) if part == 0 else (tokens, tile_num * CAP)
    out_specs.append(fixed(shape))
    out_shape.append(jax.ShapeDtypeStruct(shape, BF16))
    return pl.pallas_call(
        route_kernel if part == 0 else turn_kernel,
        grid=(2,),
        in_specs=[fixed(routing.shape), block, block],
        out_specs=out_specs,
        out_shape=out_shape,
        scratch_shapes=[pltpu.VMEM((tile_num * GROUP, HEAD_WIDTH), F32)],
        compiler_params=pltpu.CompilerParams(vmem_limit_bytes=LIMIT),
        cost_estimate=pl.CostEstimate(flops=10**9, bytes_accessed=3 * 10**6, transcendentals=0),
        name="dispatch",
    )(routing, queries, output_gradient)


def combine_kernel(turned_ref, back_ref, *refs):
    attended_ref, query_grad_ref, ninth_ref = refs[-3:]
    tile_num = back_ref.shape[0]
    for t in range(tile_num):
        last = back_ref[t, MAIN * GROUP :, :].astype(F32)
        ninth_ref[0, t * GROUP : (t + 1) * GROUP, :] = last[:, :HEAD_WIDTH]
        ninth_ref[1, t * GROUP : (t + 1) * GROUP, :] = last[:, HEAD_WIDTH:]
    for h in range(GROUP):
        lanes = slice(h * HEAD_WIDTH, (h + 1) * HEAD_WIDTH)
        parts = [back_ref[t, h * MAIN : (h + 1) * MAIN, :].astype(F32) for t in range(tile_num)]
        main = jnp.concatenate(parts, axis=0)
        for side, target in ((0, attended_ref), (1, query_grad_ref)):
            ninth = ninth_ref[side, pl.ds(h, tile_num, stride=GROUP), :]
            half = main[:, side * HEAD_WIDTH : (side + 1) * HEAD_WIDTH]
            rows = jnp.concatenate([half, ninth], axis=0).astype(BF16)
            target[:, lanes] = jnp.dot(
                turned_ref[...], rows, preferred_element_type=F32
            ).astype(BF16)


def combine(turned, back, part, earlier, shape):
    tokens = shape[0]
    tile_num = back.shape[0] // 2
    width = GROUP * HEAD_WIDTH
    block = pl.BlockSpec((tokens, width), lambda i: (0, 2 * i + part))
    whole = pl.BlockSpec(memory_space=pl.ANY)
    return pl.pallas_call(
        combine_kernel,
        grid=(2,),
        in_specs=[
            pl.BlockSpec(turned.shape, lambda i: (0, 0)),
            pl.BlockSpec((tile_num, CAP * GROUP, 2 * HEAD_WIDTH), lambda i: (i, 0, 0)),
        ]
        + [whole] * len(earlier),
        out_specs=[block, block],
        out_shape=[jax.ShapeDtypeStruct(shape, BF16)] * 2,
        scratch_shapes=[pltpu.VMEM((2, tile_num * GROUP, HEAD_WIDTH), F32)],
        input_output_aliases={2: 0, 3: 1} if earlier else {},
        compiler_params=pltpu.CompilerParams(vmem_limit_bytes=SMALL),
        cost_estimate=pl.CostEstimate(flops=10**6, bytes_accessed=10**5, transcendentals=0),
        name="combine",
    )(turned, back, *earlier)


def attend_kernel(info, rows_ref, key_ref, value_ref, back_ref, *refs, ways, depth):
    scratch = refs[-(10 + sum(TURNS)) :]
    shares = refs[: -len(scratch)]
    query_s, grad_s, out_s, query_grad_s, key_fill, key_zero, value_ones = scratch[:7]
    key_grad_s, value_grad_s, grads_s = scratch[7:10]
    buffers = list(scratch[10:])
    turns = [[buffers.pop(0) for _ in range(turn)] for turn in TURNS]
    score_s, prob_s, slope_s = ([turn[w % len(turn)] for w in range(ways)] for turn in turns)
    device_num, slot_rows, _ = rows_ref.shape
    patches = key_ref.shape[1]
    width = HEAD_WIDTH
    block_rows = query_s.shape[0] // ways
    inv_root = 1.0 / math.sqrt(width)
    to_power = math.log2(math.e) * inv_root

    live = lax.broadcasted_iota(jnp.int32, (patches, width), 0) < info[2]
    key, value = key_ref[0].astype(F32), value_ref[0].astype(F32)
    key_fill[...] = jnp.where(live, key, key[0:1, :]).astype(BF16)
    key_zero[...] = jnp.where(live, key, 0.0).astype(BF16)
    value_ones[:, :width] = jnp.where(live, value, 0.0).astype(BF16)
    value_ones[:, width:] = jnp.where(live, 1.0, 0.0).astype(BF16)
    for i in range(0, device_num, 2):
        for first, target in ((0, query_s), (width, grad_s)):
            pair = [rows_ref[i + j, :, first : first + width].astype(F32) for j in range(2)]
            target[i * slot_rows : (i + 2) * slot_rows, :] = jnp.concatenate(pair, axis=0).astype(BF16)
    key_grad_s[...] = jnp.zeros_like(key_grad_s)
    value_grad_s[...] = jnp.zeros_like(value_grad_s)

    here = [slice(w * block_rows, (w + 1) * block_rows) for w in range(ways)]
    peak, grad, grad_dot = {}, {}, {}

    def scores(w):
        score = lax.dot_general(
            query_s[here[w], :], key_fill[...], ROWS_LAST, preferred_element_type=F32
        )
        score_s[w][...] = score
        peak[w] = jnp.max(score, axis=1, keepdims=True) * to_power

    def weights(w):
        prob_s[w][...] = jnp.exp2(score_s[w][...] * to_power - peak[w]).astype(BF16)

    def output(w):
        mixed = jnp.dot(prob_s[w][...], value_ones[...], preferred_element_type=F32)
        scale = 1.0 / mixed[:, width:]
        attended = (mixed[:, :width] * scale).astype(BF16).astype(F32)
        out_s[here[w], :] = attended
        grad[w] = (grad_s[here[w], :].astype(F32) * scale).astype(BF16)
        grad_dot[w] = jnp.sum(grad[w].astype(F32) * attended, axis=1, keepdims=True)

    def slopes(w):
        prob_grad = lax.dot_general(
            grad[w], value_ones[:, :width], ROWS_LAST, preferred_element_type=F32
        )
        slope_s[w][...] = (prob_grad - grad_dot[w]).astype(BF16) * prob_s[w][...]

    def value_term(w):
        turned = grad[w].astype(F32).T.astype(BF16)
        value_grad_s[...] += jnp.dot(turned, prob_s[w][...], preferred_element_type=F32)

    def query_term(w):
        query_grad_s[here[w], :] = inv_root * jnp.dot(
            slope_s[w][...], key_zero[...], preferred_element_type=F32
        )

    def key_term(w):
        turned = query_s[here[w], :].astype(F32).T.astype(BF16)
        key_grad_s[...] += jnp.dot(turned, slope_s[w][...], preferred_element_type=F32)

    steps = (scores, weights, output, slopes, value_term, query_term, key_term)
    for now in range(len(steps) + ways - 1):
        for w in range(ways):
            if 0 <= now - w < len(steps):
                steps[now - w](w)

    for i in range(device_num):
        own = slice(i * slot_rows, (i + 1) * slot_rows)
        back_ref[i, :, :width] = out_s[own, :].astype(BF16)
        back_ref[i, :, width:] = query_grad_s[own, :].astype(BF16)
    live = lax.broadcasted_iota(jnp.int32, (width, patches), 1) < info[2]
    grads_s[:, :width] = jnp.where(live, key_grad_s[...] * inv_root, 0.0).T
    grads_s[:, width:] = jnp.where(live, value_grad_s[...], 0.0).T
    for i, share in enumerate(shares):
        size = share.shape[0]
        split = len(shares) // depth
        place = lax.rem(info[1] + i // split, depth) * split
        if split == 2:
            place = place + (info[0] if i % 2 == 0 else 1 - info[0])
        share[...] = grads_s[pl.ds(pl.multiple_of(place * size, size), size), :].astype(BF16)


def attend(info, rows, keys, values, depth, split):
    device_num, slot_rows, both = rows.shape
    patches = keys.shape[1]
    share_num = depth * split
    total = device_num * slot_rows
    width = HEAD_WIDTH
    share = patches // share_num
    ways = WAYS
    block_rows = total // ways
    tile = pl.BlockSpec((1, patches, width), lambda i, info: (0, 0, 0))
    whole = pl.BlockSpec(rows.shape, lambda i, info: (0, 0, 0))
    return pl.pallas_call(
        functools.partial(attend_kernel, ways=ways, depth=depth),
        grid_spec=pltpu.PrefetchScalarGridSpec(
            num_scalar_prefetch=1,
            grid=(1,),
            in_specs=[whole, tile, tile],
            out_specs=[whole] + [pl.BlockSpec((share, both), lambda i, info: (0, 0))] * share_num,
            scratch_shapes=[
                pltpu.VMEM((total, width), BF16),
                pltpu.VMEM((total, width), BF16),
                pltpu.VMEM((total, width), F32),
                pltpu.VMEM((total, width), F32),
                pltpu.VMEM((patches, width), BF16),
                pltpu.VMEM((patches, width), BF16),
                pltpu.VMEM((patches, both), BF16),
                pltpu.VMEM((width, patches), F32),
                pltpu.VMEM((width, patches), F32),
                pltpu.VMEM((patches, both), F32),
            ]
            + [pltpu.VMEM((block_rows, patches), F32)] * TURNS[0]
            + [pltpu.VMEM((block_rows, patches), BF16)] * (TURNS[1] + TURNS[2]),
        ),
        out_shape=[pltpu.HBM(rows.shape, BF16)] + [pltpu.HBM((share, both), BF16)] * share_num,
        compiler_params=pltpu.CompilerParams(vmem_limit_bytes=ATTEND_LIMITS[split - 1]),
        cost_estimate=pl.CostEstimate(
            flops=60 * total * patches * width,
            bytes_accessed=4 * 10**6,
            transcendentals=total * patches,
        ),
        name="attend",
    )(info, rows, keys, values)


def add_kernel(info, *refs):
    shares, (mine_ref, theirs_ref) = refs[:-2], refs[-2:]
    half = mine_ref.shape[0]
    for target, core in ((mine_ref, info[0]), (theirs_ref, 1 - info[0])):
        rows = pl.ds(pl.multiple_of(core * half, half), half)
        target[...] = sum(share[rows, :].astype(F32) for share in shares).astype(target.dtype)


def add_shares(info, shares):
    rows, both = shares[0].shape
    half = rows // 2
    fixed = lambda size: pl.BlockSpec((size, both), lambda i, info: (0, 0))
    return pl.pallas_call(
        add_kernel,
        grid_spec=pltpu.PrefetchScalarGridSpec(
            num_scalar_prefetch=1,
            grid=(1,),
            in_specs=[fixed(rows)] * len(shares),
            out_specs=[fixed(half)] * 2,
        ),
        out_shape=[jax.ShapeDtypeStruct((half, both), dtype) for dtype in (F32, BF16)],
        compiler_params=pltpu.CompilerParams(vmem_limit_bytes=SMALL),
        cost_estimate=pl.CostEstimate(flops=10**6, bytes_accessed=10**5, transcendentals=0),
        name="add_shares",
    )(info, *shares)


def place_kernel(info, *refs):
    (mine, other, *shares), (key_ref, value_ref) = refs[:-2], refs[-2:]
    width = HEAD_WIDTH
    parts = [(mine[...], other[...].astype(F32))]
    parts.append([sum(share[...].astype(F32) for share in shares[i::2]) for i in range(2)])
    for part, (own, theirs) in enumerate(parts):
        for core in range(2):
            chosen = jnp.where(info[0] == core, own, theirs)
            group = 2 * core + part
            for first, target in ((0, key_ref), (width, value_ref)):
                target[0, :, group * width : (group + 1) * width] = chosen[:, first : first + width]


def place(info, mine, other, shares):
    rows, both = mine.shape
    out = (1, rows, 2 * both)
    return pl.pallas_call(
        place_kernel,
        grid_spec=pltpu.PrefetchScalarGridSpec(
            num_scalar_prefetch=1,
            grid=(1,),
            in_specs=[pl.BlockSpec((rows, both), lambda i, info: (0, 0))] * (2 + len(shares)),
            out_specs=[pl.BlockSpec(out, lambda i, info: (0, 0, 0))] * 2,
        ),
        out_shape=[jax.ShapeDtypeStruct(out, F32)] * 2,
        compiler_params=pltpu.CompilerParams(vmem_limit_bytes=SMALL),
        cost_estimate=pl.CostEstimate(flops=10**6, bytes_accessed=10**5, transcendentals=0),
        name="place",
    )(info, mine, other, *shares)


def local(queries, tile_ids, keys, values, patch_counts, output_gradient):
    tile_num = lax.axis_size("img")
    depth = lax.axis_size("z")
    info = jnp.stack([lax.axis_index("core"), lax.axis_index("z"), patch_counts[0]]).astype(jnp.int32)
    exchange = functools.partial(
        lax.all_to_all, axis_name=("core", "img"), split_axis=0, concat_axis=0, tiled=True
    )
    ids = tile_ids.reshape(1, -1)
    sent, slots = dispatch(ids, queries, output_gradient, 0, tile_num)
    later, turned = dispatch(slots, queries, output_gradient, 1, tile_num)
    first = 2 * lax.axis_index("core") * HEAD_WIDTH
    tiles = [
        [lax.dynamic_slice_in_dim(a, first + part * HEAD_WIDTH, HEAD_WIDTH, 2) for a in (keys, values)]
        for part in range(2)
    ]
    rows, later, tiles = lax.optimization_barrier((exchange(sent), later, tiles))
    rows = [rows, exchange(later)]
    back, *shares = attend(info, rows[0], *tiles[0], depth, 1)
    first_back = exchange(back)
    along_z = lambda share, i: lax.ppermute(share, "z", [(z, (z + i) % depth) for z in range(depth)])
    early, late = ((1, 3), (2,))
    for i in early:
        shares[i] = along_z(shares[i], i)
    waiting, rows = lax.optimization_barrier(([shares[i] for i in late], rows))
    for i, share in zip(late, waiting):
        shares[i] = along_z(share, i)
    back, *later = attend(info, rows[1], *tiles[1], depth, 2)
    back, shares = lax.optimization_barrier((back, shares))
    second_back = exchange(back)
    for i in range(1, 2 * depth):
        to = lambda z, core: ((z + i // 2) % depth) * 2 + (core + i) % 2
        pairs = [(2 * z + core, to(z, core)) for z in range(depth) for core in range(2)]
        later[i] = lax.ppermute(later[i], ("z", "core"), pairs)
    mine, given = add_shares(info, shares)
    other = lax.ppermute(given, "core", [(0, 1), (1, 0)])
    outputs = combine(turned, first_back, 0, (), queries.shape)
    grads = place(info, mine, other, later)
    outputs = combine(turned, second_back, 1, outputs, queries.shape)
    return (*outputs, *grads)


def solution(mesh):
    ctx, img = mesh.devices.shape
    fine = Mesh(mesh.devices.reshape(ctx // 2, 2, img), ("z", "core", "img"))
    rows = P(("z", "core", "img"), None)
    grads = P("img", ("z", "core"), None)
    tiles = P("img", None, None)
    return jax.shard_map(
        local,
        mesh=fine,
        in_specs=(rows, rows, tiles, tiles, P("img"), rows),
        out_specs=(rows, rows, grads, grads),
        check_vma=False,
    )
```
